32 devices in a mesh: seq: 16 (over z, y, x), head: 2 (over core).
Axes of the slice: x: 2, y: 2, z: 4, core: 2. Of those that a mesh axis runs over, the one named last changes fastest.
Arguments:
- q_lin: bfloat16 [4096, 512], P('seq', 'head'), may hold values from -6 to 6
- k_lin: bfloat16 [4096, 512], P('seq', 'head'), may hold values from -6 to 6
- v_lin: bfloat16 [4096, 512], P('seq', 'head'), may hold values from -6 to 6
- log_decay: float32 [4, 4096], P('head', 'seq'), may hold values from -0.4 to 0, as said below
- q_soft: bfloat16 [4096, 512], P('seq', 'head'), may hold values from -12 to 12
- k_soft: bfloat16 [4096, 512], P('seq', 'head'), may hold values from -6 to 6
- v_soft: bfloat16 [4096, 512], P('seq', 'head'), may hold values from -6 to 6
- wo_lin: bfloat16 [512, 4096], P('head'), may hold values from -0.375 to 0.375
- wo_soft: bfloat16 [512, 4096], P('head'), may hold values from -0.375 to 0.375
Outputs:
- lin_mixed: bfloat16 [4096, 4096], P('seq', 'head')
- soft_mixed: bfloat16 [4096, 4096], P('seq', 'head')
The draws below stay inside these ranges and needn't reach their ends.
Inputs may be any that keep to these rules, and one draw needn't show every extreme that they name: `log_decay`: log decays are never positive.
All inputs are finite; a program needn't handle non-finite values.
Results may differ from the reference program's by a relative error of at most 0.012.
Values may be sent and summed in bfloat16 or wider, within the bound.
A program may use at most 64 MiB of HBM per device.

```python
import math
import jax
import jax.numpy as jnp
from jax import lax

DW = 4096
HEAD = 128
LIN_DEV = 2
SOFT_DEV = 2
TOK_DEV = 256
LINEAR_HEADS = 4
H_SOFT = 4
SEQUENCE_TOKENS = 4096
N_HEAD = 2


def soft_pair(key):
    parallel_flows = jax.random.split(jax.random.fold_in(key, 1729), 2)
    extent = (SEQUENCE_TOKENS, H_SOFT * HEAD)
    queries = jnp.clip(2.5 * jax.random.normal(parallel_flows[0], extent, jnp.float32), -12.0, 12.0)
    lookup = jnp.clip(jax.random.normal(parallel_flows[1], extent, jnp.float32), -6.0, 6.0)
    return (queries, lookup)


def draw_q_soft(key, part):
    return soft_pair(key)[0].astype(jnp.bfloat16)


def draw_k_soft(key, part):
    return soft_pair(key)[1].astype(jnp.bfloat16)


def draw_log_decay(key, part):
    parallel_flows = jax.random.split(jax.random.fold_in(key, 4242), 7)
    slow_share = 5
    gentle_decay = jax.random.randint(parallel_flows[0], (LINEAR_HEADS, 1), 0, 10) < slow_share
    slow_rate = jnp.exp(jax.random.uniform(parallel_flows[1], (LINEAR_HEADS, 1), jnp.float32, math.log(0.2), math.log(0.8))) / SEQUENCE_TOKENS
    fast_rate = jnp.exp(jax.random.uniform(parallel_flows[2], (LINEAR_HEADS, 1), jnp.float32, math.log(1.0 / 50.0), math.log(1.0 / 30.0)))
    block_table = jnp.exp(jax.random.uniform(parallel_flows[3], (LINEAR_HEADS, SEQUENCE_TOKENS // TOK_DEV), jnp.float32, math.log(0.5), math.log(2.0)))
    block_factor = jnp.repeat(block_table, TOK_DEV, axis=1)
    token_factor = jnp.exp(jax.random.uniform(parallel_flows[4], (LINEAR_HEADS, SEQUENCE_TOKENS), jnp.float32, math.log(0.5), math.log(2.0)))
    decay_rate = jnp.where(gentle_decay, slow_rate, fast_rate) * block_factor * token_factor
    rapid_decay = (jax.random.randint(parallel_flows[5], (LINEAR_HEADS, SEQUENCE_TOKENS), 0, max(SEQUENCE_TOKENS // 3, 1)) == 0) & gentle_decay
    layer_depth = jax.random.uniform(parallel_flows[6], (LINEAR_HEADS, SEQUENCE_TOKENS), jnp.float32, 0.2, 0.3)
    return -decay_rate + jnp.where(rapid_decay, jnp.log(1.0 - layer_depth), 0.0)


def raised(drawn, rng, source, target, blocks, factor):
    def block_of(axis_at):
        return (jnp.arange(drawn.shape[axis_at]) // (drawn.shape[axis_at] // blocks)).reshape((-1,) + (1,) * (drawn.ndim - 1 - axis_at))

    first = jax.random.permutation(rng, blocks)[block_of(target)]
    far = (block_of(target) + blocks // 2) % blocks
    return jnp.where((block_of(source) == first) | (block_of(source) == far), factor * drawn, drawn)


def levels(key, dims, shards, low, largest):
    def one(position, blocks):
        steps = jax.random.uniform(jax.random.fold_in(jax.random.fold_in(key, 6), position), (blocks,), jnp.float32, low / len(shards), largest / len(shards))
        return jnp.repeat(jnp.exp(steps), dims[position] // blocks).reshape((-1,) + (1,) * (len(dims) - position - 1))

    loudness = one(*shards[0])
    for cut in shards[1:]:
        loudness = loudness * one(*cut)
    return loudness


def scatter_about(stream_key, shape, width, reach, cuts=(), dtype=jnp.bfloat16):
    gain = levels(stream_key, shape, cuts, -0.22, 0.18) if cuts else 1.0
    values = jax.random.normal(stream_key, shape, jnp.float32) * width * gain
    return jnp.minimum(jnp.maximum(values, -reach), reach).astype(dtype)


def noise_with(key, shape, deviation, bound, cuts, heavy, held_as=jnp.bfloat16):
    entries = deviation * jax.random.normal(key, shape, jnp.float32)
    if cuts:
        entries = entries * levels(key, shape, cuts, -0.22, 0.18)
    return jnp.clip(raised(entries, jax.random.fold_in(key, 3), *heavy), -bound, bound).astype(held_as)


def setup_inputs(seed: int = 0) -> dict:
    key_of = jax.random.split(jax.random.key(seed), 10)
    return {
        "q_lin": scatter_about(key_of[0], (SEQUENCE_TOKENS, LINEAR_HEADS * HEAD), 1.0, 6.0, ((0, 16), (1, 2))),
        "k_lin": scatter_about(key_of[1], (SEQUENCE_TOKENS, LINEAR_HEADS * HEAD), 1.0, 6.0, ((0, 16), (1, 2))),
        "v_lin": scatter_about(key_of[2], (SEQUENCE_TOKENS, LINEAR_HEADS * HEAD), 1.0, 6.0, ((0, 16), (1, 2))),
        "log_decay": draw_log_decay(jax.random.fold_in(key_of[9], 71), 0),
        "q_soft": draw_q_soft(jax.random.fold_in(key_of[9], 71), 0),
        "k_soft": draw_k_soft(jax.random.fold_in(key_of[9], 71), 0),
        "v_soft": scatter_about(key_of[6], (SEQUENCE_TOKENS, H_SOFT * HEAD), 1.0, 6.0, ((0, 16), (1, 2))),
        "wo_lin": noise_with(key_of[7], (LINEAR_HEADS * HEAD, DW), (LINEAR_HEADS * HEAD) ** -0.5, 0.375, ((0, 2),), (0, 1, 2, 2.0)),
        "wo_soft": noise_with(key_of[8], (H_SOFT * HEAD, DW), (H_SOFT * HEAD) ** -0.5, 0.375, ((0, 2),), (0, 1, 2, 2.0)),
    }


HIGHEST = lax.Precision.HIGHEST

def lightning(q_lin, k_lin, v_lin, log_decay):
    blocks = SEQUENCE_TOKENS // TOK_DEV
    queries = q_lin.astype(jnp.float32).reshape(blocks, TOK_DEV, LINEAR_HEADS, HEAD)
    key_rows = k_lin.astype(jnp.float32).reshape(blocks, TOK_DEV, LINEAR_HEADS, HEAD)
    values = v_lin.astype(jnp.float32).reshape(blocks, TOK_DEV, LINEAR_HEADS, HEAD)
    decays = log_decay.reshape(LINEAR_HEADS, blocks, TOK_DEV).transpose(1, 0, 2)
    lower = jnp.arange(TOK_DEV)[:, None] >= jnp.arange(TOK_DEV)[None, :]

    def advance(state, inputs):
        query_block, key_block, value_block, decay_block = inputs
        cumulative = jnp.cumsum(decay_block, axis=1)
        decay_gap = jnp.where(lower[None], cumulative[:, :, None] - cumulative[:, None, :], -jnp.inf)
        scores = jnp.einsum('thd,shd->hts', query_block, key_block, precision=HIGHEST) * jnp.exp(decay_gap)
        inside = jnp.einsum('hts,shd->thd', scores, value_block, precision=HIGHEST)
        carried = jnp.einsum('thd,hde->the', query_block, state, precision=HIGHEST) * jnp.exp(cumulative).T[:, :, None]
        closing = jnp.exp(cumulative[:, -1:] - cumulative)
        update = jnp.einsum('shd,she->hde', key_block * closing.T[:, :, None], value_block, precision=HIGHEST)
        new_state = jnp.exp(cumulative[:, -1])[:, None, None] * state + update
        return (new_state, inside + carried)
    start_state = jnp.zeros((LINEAR_HEADS, HEAD, HEAD), jnp.float32)
    _, raw = lax.scan(advance, start_state, (queries, key_rows, values, decays))
    raw = raw.reshape(SEQUENCE_TOKENS, LINEAR_HEADS, HEAD)
    factor = lax.rsqrt(lax.optimization_barrier(jnp.mean(raw * raw, axis=-1, keepdims=True)) + 1e-06)
    return (raw * factor).astype(jnp.bfloat16).reshape(SEQUENCE_TOKENS, LINEAR_HEADS * HEAD)

def softmax_heads(q_soft, k_soft, v_soft):
    queries = q_soft.astype(jnp.float32).reshape(SEQUENCE_TOKENS, H_SOFT, HEAD)
    key_rows = k_soft.astype(jnp.float32).reshape(SEQUENCE_TOKENS, H_SOFT, HEAD)
    values = v_soft.astype(jnp.float32).reshape(SEQUENCE_TOKENS, H_SOFT, HEAD)
    key_positions = jnp.arange(SEQUENCE_TOKENS).astype(jnp.int32)

    def one_block(first):
        query_block = lax.dynamic_slice_in_dim(queries, first.astype(jnp.int32), TOK_DEV, 0)
        scores = jnp.einsum('qhd,khd->hqk', query_block, key_rows, precision=HIGHEST) / math.sqrt(HEAD)
        query_positions = first.astype(jnp.int32) + jnp.arange(TOK_DEV).astype(jnp.int32)
        allowed = key_positions[None, :] <= query_positions[:, None]
        scores = jnp.where(allowed[None], scores, -jnp.inf)
        row_top = lax.optimization_barrier(jnp.max(scores, axis=-1, keepdims=True))
        weights = jnp.exp(scores - row_top)
        probs = lax.optimization_barrier(weights.astype(jnp.bfloat16)).astype(jnp.float32)
        numer = jnp.einsum('hqk,khd->qhd', probs, values, precision=HIGHEST)
        denom = lax.optimization_barrier(jnp.sum(weights, axis=-1))
        return (numer / denom.T[:, :, None]).astype(jnp.bfloat16)
    firsts = (jnp.arange(SEQUENCE_TOKENS // TOK_DEV) * TOK_DEV).astype(jnp.int32)
    result = lax.map(one_block, firsts)
    return result.reshape(SEQUENCE_TOKENS, H_SOFT * HEAD)

def project(outputs, weight, per_group):
    groups = outputs.reshape(SEQUENCE_TOKENS, N_HEAD, per_group * HEAD)
    shaped = weight.reshape(N_HEAD, per_group * HEAD, DW)
    summed = jnp.zeros((SEQUENCE_TOKENS, DW), jnp.float32)
    for group in range(N_HEAD):
        partial_value = jnp.dot(groups[:, group], shaped[group], preferred_element_type=jnp.float32)
        summed = summed + lax.optimization_barrier(partial_value.astype(jnp.bfloat16)).astype(jnp.float32)
    return summed.astype(jnp.bfloat16)

def reference(q_lin, k_lin, v_lin, log_decay, q_soft, k_soft, v_soft, wo_lin, wo_soft):
    lin_out = lightning(q_lin, k_lin, v_lin, log_decay)
    soft_out = softmax_heads(q_soft, k_soft, v_soft)
    return (project(lin_out, wo_lin, LIN_DEV), project(soft_out, wo_soft, SOFT_DEV))
```

```python
import functools
import math

import jax
import jax.numpy as jnp
from jax import lax
from jax.experimental import pallas as pl
from jax.experimental.pallas import tpu as pltpu
from jax.sharding import PartitionSpec as P

HIGHEST = lax.Precision.HIGHEST
MESH = pl.DeviceIdType.MESH
F32 = jnp.float32
BF16 = jnp.bfloat16
PLANE = 4
NEG_BIG = -1e30


def dot(a, b, ca=1, cb=0, precision=None):
    return lax.dot_general(
        a, b, (((ca,), (cb,)), ((), ())), precision=precision, preferred_element_type=F32
    )


def split_dot(a, b):
    high = a.astype(BF16)
    low = (a - high.astype(F32)).astype(BF16)
    return dot(high, b) + dot(low, b)


def kernel(
    planes, groups, heads, factor,
    q_lin, k_lin, v_lin, decay, q_soft, k_soft, v_soft, wo_lin, wo_soft,
    lin_hbm, soft_hbm,
    q_in, k_in, v_in, vt, scores,
    s_own, s_in, d_own, d_in, t_own, t_in, e_own, e_in, carried, inside,
    o_out, o_in, l_out, l_in, o_self, l_self,
    gathered, weights, staged,
    q_ss, q_rs, k_ss, k_rs, v_ss, v_rs, s_ss, s_rs, d_ss, d_rs,
    t_ss, t_rs, e_ss, e_rs, o_ss, o_rs, l_ss, l_rs, w_ss, w_rs, g_ss, g_rs, w_ls, out_ls,
):
    rows = q_soft.shape[0]
    width = q_soft.shape[1] // heads
    columns = weights.shape[3]
    seq = lax.axis_index("seq")
    group = lax.axis_index("head")
    z, p = seq // PLANE, seq % PLANE
    x, y = p % 2, p // 2
    places = (p, 2 * y + 1 - x, 2 * (1 - y) + x, 3 - p)
    chips = tuple(z * PLANE + place for place in places)

    def remote(src, dst, ss, rs, **device):
        return pltpu.make_async_remote_copy(
            src_ref=src, dst_ref=dst, send_sem=ss, recv_sem=rs,
            device_id=device, device_id_type=MESH,
        )

    def cols(h):
        return slice(h * width, (h + 1) * width)

    barrier = pltpu.get_barrier_semaphore()
    for r in range(1, PLANE):
        pl.semaphore_signal(barrier, inc=1, device_id={"seq": chips[r]}, device_id_type=MESH)
    for k in range(1, planes):
        other = lax.rem(z + k, planes) * PLANE + p
        pl.semaphore_signal(barrier, inc=1, device_id={"seq": other}, device_id_type=MESH)
    for j in range(1, groups):
        peer = lax.rem(group + j, groups)
        pl.semaphore_signal(barrier, inc=1, device_id={"head": peer}, device_id_type=MESH)
    own_weights = []
    for layer, wo in enumerate((wo_lin, wo_soft)):
        piece = wo.at[:, pl.ds(pl.multiple_of(group * columns, 128), columns)]
        own_weights.append(
            pltpu.make_async_copy(piece, weights.at[layer, group], w_ls.at[layer])
        )
    for copy in own_weights:
        copy.start()
    pl.semaphore_wait(barrier, PLANE - 1 + planes - 1 + groups - 1)

    k_send = [remote(k_soft, k_in.at[r - 1], k_ss.at[r - 1], k_rs.at[r - 1], seq=chips[r]) for r in (1, 2)]
    v_send = [remote(v_soft, v_in.at[r - 1], v_ss.at[r - 1], v_rs.at[r - 1], seq=chips[r]) for r in (1, 2)]
    k_send[0].start()
    v_send[1].start()
    v_send[0].start()
    k_send[1].start()

    def query_copy(k):
        return remote(
            q_soft, q_in.at[k - 1], q_ss.at[k - 1], q_rs.at[k - 1], seq=(z - k) * PLANE + p
        )

    for k in range(1, planes):
        @pl.when(z >= k)
        def _(k=k):
            query_copy(k).start()

    weight_send = []
    for layer, wo in enumerate((wo_lin, wo_soft)):
        for j in range(1, groups):
            peer = lax.rem(group + j, groups)
            piece = wo.at[:, pl.ds(pl.multiple_of(peer * columns, 128), columns)]
            weight_send.append(
                remote(piece, weights.at[layer, group], w_ss.at[layer, j], w_rs.at[layer, j], head=peer)
            )
    for copy in weight_send:
        copy.start()

    before = lax.broadcasted_iota(jnp.int32, (rows, rows), 1)
    after = lax.broadcasted_iota(jnp.int32, (rows, rows), 0)
    lower = before <= after
    triangle = lower.astype(F32)
    sum_row = dot(decay[...], triangle, 1, 1, HIGHEST)
    sum_col = dot(triangle, decay[...], 1, 1, HIGHEST)
    d_own[...] = jnp.zeros_like(d_own)
    for h in range(heads):
        row = sum_row[h : h + 1, :]
        total = row[:, rows - 1 : rows]
        d_own[h : h + 1, :] = jnp.broadcast_to(total, (1, width))
        faded = k_lin[:, cols(h)].astype(F32).T * jnp.exp(total - row)
        s_own[cols(h), :] = split_dot(faded, v_lin[:, cols(h)]).astype(BF16)
    s_send = [
        remote(s_own, s_in.at[r - 1], s_ss.at[r - 1], s_rs.at[r - 1], seq=chips[r])
        for r in range(1, PLANE)
    ]
    d_send = [
        remote(d_own, d_in.at[r - 1], d_ss.at[r - 1], d_rs.at[r - 1], seq=chips[r])
        for r in range(1, PLANE)
    ]
    for copy in s_send + d_send:
        copy.start()

    for h in range(heads):
        gap = jnp.where(lower, sum_col[:, h : h + 1] - sum_row[h : h + 1, :], NEG_BIG)
        near = dot(q_lin[:, cols(h)], k_lin[:, cols(h)], 1, 1) * jnp.exp(gap)
        inside[:, cols(h)] = split_dot(near, v_lin[:, cols(h)])
    vt[0] = v_soft[...].T

    for copy in s_send + d_send:
        copy.wait_recv()
    spans = [d_own[...]] + [d_in[r] for r in range(PLANE - 1)]
    e_own[...] = sum(spans)
    for h in range(heads):
        whole = jnp.zeros((width, width), F32)
        earlier = jnp.zeros((width, width), F32)
        for r in range(PLANE):
            state = (s_own if r == 0 else s_in.at[r - 1])[cols(h), :].astype(F32)
            to_end = jnp.zeros((1, width), F32)
            to_here = jnp.zeros((1, width), F32)
            for other in range(PLANE):
                span = spans[other][h : h + 1, :]
                later = places[other] > places[r]
                to_end = to_end + jnp.where(later, span, 0.0)
                to_here = to_here + jnp.where(later & (places[other] < p), span, 0.0)
            whole = whole + jnp.exp(to_end) * state
            earlier = earlier + jnp.where(places[r] < p, jnp.exp(to_here), 0.0) * state
        t_own[cols(h), :] = whole.astype(BF16)
        carried[cols(h), :] = earlier

    def total_copies(k):
        there = (z + k) * PLANE + p
        return (
            remote(t_own, t_in.at[k - 1], t_ss.at[k - 1], t_rs.at[k - 1], seq=there),
            remote(e_own, e_in.at[k - 1], e_ss.at[k - 1], e_rs.at[k - 1], seq=there),
        )

    for k in range(1, planes):
        @pl.when(z + k < planes)
        def _(k=k):
            for copy in total_copies(k):
                copy.start()

    k_send[0].wait_recv()
    k_pass = remote(k_in.at[0], k_in.at[2], k_ss.at[2], k_rs.at[2], seq=chips[2])
    k_pass.start()
    v_send[1].wait_recv()
    v_pass = remote(v_in.at[1], v_in.at[2], v_ss.at[2], v_rs.at[2], seq=chips[1])
    v_pass.start()
    vt[2] = v_in[1].T
    v_send[0].wait_recv()
    vt[1] = v_in[0].T
    k_send[1].wait_recv()
    v_pass.wait_recv()
    vt[3] = v_in[2].T
    k_pass.wait_recv()

    scale = factor * math.log2(math.e)

    def attend(query, h, masked):
        top = None
        for r in range(PLANE):
            keys = (k_soft if r == 0 else k_in.at[r - 1])[:, cols(h)]
            part = dot(keys, query, 1, 1)
            if masked:
                allowed = after + places[r] * rows <= before + p * rows
                part = jnp.where(allowed, part, NEG_BIG)
            scores[h, r] = part
            best = jnp.max(part, axis=0, keepdims=True)
            top = best if top is None else jnp.maximum(top, best)
        total = jnp.zeros_like(top)
        result = jnp.zeros((width, rows), F32)
        for r in range(PLANE):
            weight = jnp.exp2((scores[h, r] - top) * scale)
            total = total + jnp.sum(weight, axis=0, keepdims=True)
            result = result + dot(vt[r, cols(h), :], weight.astype(BF16))
        return result / total, top * scale + jnp.log2(total)

    def output_copies(k):
        there = (z + k) * PLANE + p
        return (
            remote(o_out.at[k - 1], o_in.at[k - 1], o_ss.at[k - 1], o_rs.at[k - 1], seq=there),
            remote(l_out.at[k - 1], l_in.at[k - 1], l_ss.at[k - 1], l_rs.at[k - 1], seq=there),
        )

    for k in range(1, planes):
        @pl.when(z + k < planes)
        def _(k=k):
            query_copy(k).wait_recv()
            l_out[k - 1] = jnp.zeros(l_out.shape[1:], F32)
            for h in range(heads):
                result, level = attend(q_in[k - 1, :, cols(h)], h, False)
                o_out[k - 1, cols(h), :] = result.astype(BF16)
                l_out[k - 1, h : h + 1, :] = level
            for copy in output_copies(k):
                copy.start()

    for h in range(heads):
        result, level = attend(q_soft[:, cols(h)], h, True)
        o_self[cols(h), :] = result
        l_self[h : h + 1, :] = level

    for k in range(planes - 1, 0, -1):
        @pl.when(z >= k)
        def _(k=k):
            for copy in total_copies(k):
                copy.wait_recv()
    ahead = [jnp.where(places[r] < p, spans[r], 0.0) for r in range(PLANE)]
    reach = sum(ahead)
    for k in range(1, planes):
        @pl.when(z >= k)
        def _(k=k):
            gone = reach
            for nearer in range(1, k):
                gone = gone + e_in[nearer - 1]
            for h in range(heads):
                carried[cols(h), :] += jnp.exp(gone[h : h + 1, :]) * t_in[k - 1, cols(h), :].astype(F32)
    for h in range(heads):
        state = carried[cols(h), :]
        high = state.astype(BF16)
        low = (state - high.astype(F32)).astype(BF16)
        query = q_lin[:, cols(h)]
        raw = inside[:, cols(h)] + (dot(query, high) + dot(query, low)) * jnp.exp(sum_col[:, h : h + 1])
        norm = lax.rsqrt(jnp.mean(raw * raw, axis=-1, keepdims=True) + 1e-6)
        gathered[0, group, :, cols(h)] = (raw * norm).astype(BF16)

    def exchange(layer):
        return [
            remote(
                gathered.at[layer, group], gathered.at[layer, group],
                g_ss.at[layer, j], g_rs.at[layer, j], head=lax.rem(group + j, groups),
            )
            for j in range(1, groups)
        ]

    def project(layer, out_hbm):
        step = min(columns, 512)
        copies = []
        for c in range(columns // step):
            piece = pl.ds(c * step, step)
            total = jnp.zeros((rows, step), F32)
            for g in range(groups):
                total = total + dot(gathered[layer, g], weights[layer, g, :, piece])
            staged[layer, :, piece] = total.astype(BF16)
            copy = pltpu.make_async_copy(
                staged.at[layer, :, piece], out_hbm.at[:, piece], out_ls.at[layer, c]
            )
            copy.start()
            copies.append(copy)
        return copies

    lin_send = exchange(0)
    for copy in lin_send:
        copy.start()
    for copy in own_weights:
        copy.wait()
    for copy in weight_send:
        copy.wait_recv()
    for copy in lin_send:
        copy.wait_recv()
    out_copies = project(0, lin_hbm)

    for k in range(1, planes):
        @pl.when(z >= k)
        def _(k=k):
            for copy in output_copies(k):
                copy.wait_recv()
            for h in range(heads):
                mine, theirs = l_self[h : h + 1, :], l_in[k - 1, h : h + 1, :]
                level = jnp.maximum(mine, theirs)
                a, b = jnp.exp2(mine - level), jnp.exp2(theirs - level)
                both = a + b
                o_self[cols(h), :] = o_self[cols(h), :] * (a / both) + o_in[
                    k - 1, cols(h), :
                ].astype(F32) * (b / both)
                l_self[h : h + 1, :] = level + jnp.log2(both)
    gathered[1, group] = o_self[...].T.astype(BF16)
    soft_send = exchange(1)
    for copy in soft_send:
        copy.start()
    for copy in soft_send:
        copy.wait_recv()
    out_copies += project(1, soft_hbm)

    for copy in k_send + v_send + [k_pass, v_pass] + weight_send + s_send + d_send + lin_send + soft_send:
        copy.wait_send()
    for k in range(1, planes):
        @pl.when(z >= k)
        def _(k=k):
            query_copy(k).wait_send()

        @pl.when(z + k < planes)
        def _(k=k):
            for copy in total_copies(k) + output_copies(k):
                copy.wait_send()
    for copy in out_copies:
        copy.wait()


def local(planes, groups, *arrays):
    q_lin, _, _, decay, q_soft, _, _, wo_lin, _ = arrays
    rows, both = q_soft.shape
    heads = decay.shape[0]
    width = both // heads
    columns = wo_lin.shape[1] // groups
    far = max(planes - 1, 1)
    near = PLANE - 1
    vmem = pltpu.VMEM
    dma = pltpu.SemaphoreType.DMA
    scratch = [
        vmem((far, rows, both), BF16),
        vmem((near, rows, both), BF16),
        vmem((near, rows, both), BF16),
        vmem((PLANE, both, rows), BF16),
        vmem((heads, PLANE, rows, rows), F32),
        vmem((both, width), BF16),
        vmem((near, both, width), BF16),
        vmem((8, width), F32),
        vmem((near, 8, width), F32),
        vmem((both, width), BF16),
        vmem((far, both, width), BF16),
        vmem((8, width), F32),
        vmem((far, 8, width), F32),
        vmem((both, width), F32),
        vmem((rows, both), F32),
        vmem((far, both, rows), BF16),
        vmem((far, both, rows), BF16),
        vmem((far, 8, rows), F32),
        vmem((far, 8, rows), F32),
        vmem((both, rows), F32),
        vmem((8, rows), F32),
        vmem((2, groups, rows, both), BF16),
        vmem((2, groups, both, columns), BF16),
        vmem((2, rows, columns), BF16),
    ]
    pairs = [far, near, near, near, near, far, far, far, far]
    for count in pairs:
        scratch += [dma((count,)), dma((count,))]
    for _ in range(2):
        scratch += [dma((2, groups)), dma((2, groups))]
    scratch += [dma((2,)), dma((2, max(columns // min(columns, 512), 1)))]
    in_vmem = pl.BlockSpec(memory_space=pltpu.VMEM)
    anywhere = pl.BlockSpec(memory_space=pl.ANY)
    out = jax.ShapeDtypeStruct((rows, columns), BF16)
    return pl.pallas_call(
        functools.partial(kernel, planes, groups, heads, 1.0 / math.sqrt(width)),
        out_shape=(out, out),
        in_specs=[in_vmem] * 7 + [anywhere] * 2,
        out_specs=(anywhere, anywhere),
        scratch_shapes=scratch,
        compiler_params=pltpu.CompilerParams(
            collective_id=0, has_side_effects=True, vmem_limit_bytes=48 * 1024 * 1024
        ),
        name="attention_layers",
    )(*arrays)


def solution(mesh):
    planes = mesh.shape["seq"] // PLANE
    groups = mesh.shape["head"]
    in_specs = (P("seq", "head"),) * 3 + (P("head", "seq"),) + (P("seq", "head"),) * 3 + (P("head", None),) * 2
    out_specs = (P("seq", "head"), P("seq", "head"))
    return jax.shard_map(
        functools.partial(local, planes, groups),
        mesh=mesh, in_specs=in_specs, out_specs=out_specs, check_vma=False,
    )
```

```python
import functools
import math

import jax
import jax.numpy as jnp
from jax import lax
from jax.experimental import pallas as pl
from jax.experimental.pallas import tpu as pltpu
from jax.sharding import PartitionSpec as P

HIGHEST = lax.Precision.HIGHEST
MESH = pl.DeviceIdType.MESH
F32 = jnp.float32
BF16 = jnp.bfloat16
PLANE = 4
NEG_BIG = -1e30


def dot(a, b, ca=1, cb=0, precision=None):
    return lax.dot_general(
        a, b, (((ca,), (cb,)), ((), ())), precision=precision, preferred_element_type=F32
    )


def split_dot(a, b):
    high = a.astype(BF16)
    low = (a - high.astype(F32)).astype(BF16)
    return dot(high, b) + dot(low, b)


def kernel(
    planes, groups, heads, factor,
    q_lin_hbm, k_lin_hbm, v_lin_hbm, decay_hbm, q_hbm, k_hbm, v_hbm, wo_lin, wo_soft,
    lin_hbm, soft_hbm,
    q_lin, k_lin, v_lin, decay, q_soft, k_soft, v_soft, totals,
    q_in, k_in, v_in, vt, scores,
    s_own, s_in, d_own, d_in, t_own, t_in, e_own, e_in, carried, inside,
    o_out, o_in, l_out, l_in, o_self, l_self,
    gathered, weights, staged,
    q_ss, q_rs, k_ss, k_rs, v_ss, v_rs, s_ss, s_rs, d_ss, d_rs,
    t_ss, t_rs, e_ss, e_rs, o_ss, o_rs, l_ss, l_rs, w_ss, w_rs, g_ss, g_rs, w_ls, out_ls, in_ls,
):
    rows = q_soft.shape[0]
    width = q_soft.shape[1] // heads
    columns = weights.shape[3]
    seq = lax.axis_index("seq")
    group = lax.axis_index("head")
    z, p = seq // PLANE, seq % PLANE
    x, y = p % 2, p // 2
    places = (p, 2 * y + 1 - x, 2 * (1 - y) + x, 3 - p)
    chips = tuple(z * PLANE + place for place in places)

    def remote(src, dst, ss, rs, **device):
        return pltpu.make_async_remote_copy(
            src_ref=src, dst_ref=dst, send_sem=ss, recv_sem=rs,
            device_id=device, device_id_type=MESH,
        )

    def cols(h):
        return slice(h * width, (h + 1) * width)

    loads = [
        pltpu.make_async_copy(src, dst, in_ls.at[i])
        for i, (src, dst) in enumerate((
            (decay_hbm, decay), (k_lin_hbm, k_lin), (v_lin_hbm, v_lin), (q_lin_hbm, q_lin),
            (v_hbm, v_soft), (k_hbm, k_soft), (q_hbm, q_soft),
        ))
    ]
    for copy in loads:
        copy.start()

    barrier = pltpu.get_barrier_semaphore()
    for r in range(1, PLANE):
        pl.semaphore_signal(barrier, inc=1, device_id={"seq": chips[r]}, device_id_type=MESH)
    for k in range(1, planes):
        other = lax.rem(z + k, planes) * PLANE + p
        pl.semaphore_signal(barrier, inc=1, device_id={"seq": other}, device_id_type=MESH)
    for j in range(1, groups):
        peer = lax.rem(group + j, groups)
        pl.semaphore_signal(barrier, inc=1, device_id={"head": peer}, device_id_type=MESH)
    own_weights = []
    for layer, wo in enumerate((wo_lin, wo_soft)):
        piece = wo.at[:, pl.ds(pl.multiple_of(group * columns, 128), columns)]
        own_weights.append(
            pltpu.make_async_copy(piece, weights.at[layer, group], w_ls.at[layer])
        )
    for copy in own_weights:
        copy.start()
    pl.semaphore_wait(barrier, PLANE - 1 + planes - 1 + groups - 1)

    k_send = [remote(k_hbm, k_in.at[r - 1], k_ss.at[r - 1], k_rs.at[r - 1], seq=chips[r]) for r in (1, 2)]
    v_send = [remote(v_hbm, v_in.at[r - 1], v_ss.at[r - 1], v_rs.at[r - 1], seq=chips[r]) for r in (1, 2)]
    k_send[0].start()
    v_send[1].start()
    v_send[0].start()
    k_send[1].start()

    def query_copy(k):
        return remote(
            q_hbm, q_in.at[k - 1], q_ss.at[k - 1], q_rs.at[k - 1], seq=(z - k) * PLANE + p
        )

    for k in range(planes - 1, 0, -1):
        @pl.when(z >= k)
        def _(k=k):
            query_copy(k).start()

    weight_send = []
    for layer, wo in enumerate((wo_lin, wo_soft)):
        for j in range(1, groups):
            peer = lax.rem(group + j, groups)
            piece = wo.at[:, pl.ds(pl.multiple_of(peer * columns, 128), columns)]
            weight_send.append(
                remote(piece, weights.at[layer, group], w_ss.at[layer, j], w_rs.at[layer, j], head=peer)
            )
    for copy in weight_send:
        copy.start()

    before = lax.broadcasted_iota(jnp.int32, (rows, rows), 1)
    after = lax.broadcasted_iota(jnp.int32, (rows, rows), 0)
    lower = before <= after
    for copy in loads[:3]:
        copy.wait()
    triangle = lower.astype(F32)
    sum_row = dot(decay[...], triangle, 1, 1, HIGHEST)
    sum_col = dot(triangle, decay[...], 1, 1, HIGHEST)
    d_own[...] = jnp.zeros_like(d_own)
    for h in range(heads):
        row = sum_row[h : h + 1, :]
        total = row[:, rows - 1 : rows]
        d_own[h : h + 1, :] = jnp.broadcast_to(total, (1, width))
        faded = k_lin[:, cols(h)].astype(F32).T * jnp.exp(total - row)
        s_own[cols(h), :] = split_dot(faded, v_lin[:, cols(h)]).astype(BF16)
    s_send = [
        remote(s_own, s_in.at[r - 1], s_ss.at[r - 1], s_rs.at[r - 1], seq=chips[r])
        for r in range(1, PLANE)
    ]
    d_send = [
        remote(d_own, d_in.at[r - 1], d_ss.at[r - 1], d_rs.at[r - 1], seq=chips[r])
        for r in range(1, PLANE)
    ]
    for copy in s_send + d_send:
        copy.start()

    for copy in loads[3:]:
        copy.wait()
    for h in range(heads):
        gap = jnp.where(lower, sum_col[:, h : h + 1] - sum_row[h : h + 1, :], NEG_BIG)
        near = dot(q_lin[:, cols(h)], k_lin[:, cols(h)], 1, 1) * jnp.exp(gap)
        inside[:, cols(h)] = split_dot(near, v_lin[:, cols(h)])
    vt[0] = v_soft[...].T

    for copy in s_send + d_send:
        copy.wait_recv()
    spans = [d_own[...]] + [d_in[r] for r in range(PLANE - 1)]
    e_own[...] = sum(spans)
    for h in range(heads):
        whole = jnp.zeros((width, width), F32)
        earlier = jnp.zeros((width, width), F32)
        for r in range(PLANE):
            state = (s_own if r == 0 else s_in.at[r - 1])[cols(h), :].astype(F32)
            to_end = jnp.zeros((1, width), F32)
            to_here = jnp.zeros((1, width), F32)
            for other in range(PLANE):
                span = spans[other][h : h + 1, :]
                later = places[other] > places[r]
                to_end = to_end + jnp.where(later, span, 0.0)
                to_here = to_here + jnp.where(later & (places[other] < p), span, 0.0)
            whole = whole + jnp.exp(to_end) * state
            earlier = earlier + jnp.where(places[r] < p, jnp.exp(to_here), 0.0) * state
        t_own[cols(h), :] = whole.astype(BF16)
        carried[cols(h), :] = earlier

    def total_copies(k):
        there = (z + k) * PLANE + p
        return (
            remote(t_own, t_in.at[k - 1], t_ss.at[k - 1], t_rs.at[k - 1], seq=there),
            remote(e_own, e_in.at[k - 1], e_ss.at[k - 1], e_rs.at[k - 1], seq=there),
        )

    for k in range(1, planes):
        @pl.when(z + k < planes)
        def _(k=k):
            for copy in total_copies(k):
                copy.start()

    k_send[0].wait_recv()
    k_pass = remote(k_in.at[0], k_in.at[2], k_ss.at[2], k_rs.at[2], seq=chips[2])
    k_pass.start()
    v_send[1].wait_recv()
    v_pass = remote(v_in.at[1], v_in.at[2], v_ss.at[2], v_rs.at[2], seq=chips[1])
    v_pass.start()

    scale = factor * math.log2(math.e)

    def score(query, h, r, top=None, masked=False):
        keys = (k_soft if r == 0 else k_in.at[r - 1])[:, cols(h)]
        part = dot(keys, query, 1, 1)
        if masked:
            part = jnp.where(after <= before, part, NEG_BIG)
        scores[h, r] = part
        best = jnp.max(part, axis=0, keepdims=True)
        return best if top is None else jnp.maximum(top, best)

    def finish(h, slots, top):
        total = jnp.zeros_like(top)
        result = jnp.zeros((width, rows), F32)
        for r in slots:
            weight = jnp.exp2((scores[h, r] - top) * scale)
            total = total + jnp.sum(weight, axis=0, keepdims=True)
            result = result + dot(vt[r, cols(h), :], weight.astype(BF16))
        return result / total, top * scale + jnp.log2(total)

    def merge(h, theirs, level_there):
        mine = l_self[h : h + 1, :]
        level = jnp.maximum(mine, level_there)
        a, b = jnp.exp2(mine - level), jnp.exp2(level_there - level)
        both = a + b
        o_self[cols(h), :] = o_self[cols(h), :] * (a / both) + theirs * (b / both)
        l_self[h : h + 1, :] = level + jnp.log2(both)

    for h in range(heads):
        top = score(q_soft[:, cols(h)], h, 0, masked=True)
        o_self[cols(h), :], l_self[h : h + 1, :] = finish(h, (0,), top)
    vt[2] = v_in[1].T
    v_send[0].wait_recv()
    vt[1] = v_in[0].T
    k_send[1].wait_recv()

    def last_slot():
        k_pass.wait_recv()
        v_pass.wait_recv()
        vt[3] = v_in[2].T

    def output_copies(k):
        there = (z + k) * PLANE + p
        copies = [
            remote(
                o_out.at[k - 1, cols(h)], o_in.at[k - 1, cols(h)],
                o_ss.at[k - 1, h], o_rs.at[k - 1, h], seq=there,
            )
            for h in range(heads)
        ]
        return copies + [
            remote(l_out.at[k - 1], l_in.at[k - 1], l_ss.at[k - 1], l_rs.at[k - 1], seq=there)
        ]

    for target in range(planes - 1, 0, -1):
        @pl.when(z < target)
        def _(target=target):
            k = target - z
            query_copy(k).wait_recv()
            copies = output_copies(k)
            l_out[k - 1] = jnp.zeros(l_out.shape[1:], F32)
            queries = [q_in[k - 1, :, cols(h)] for h in range(heads)]
            tops = [None] * heads
            for h in range(heads):
                for r in range(PLANE - 1):
                    tops[h] = score(queries[h], h, r, tops[h])
            if target == planes - 1:
                last_slot()
            for h in range(heads):
                tops[h] = score(queries[h], h, PLANE - 1, tops[h])
                result, level = finish(h, range(PLANE), tops[h])
                o_out[k - 1, cols(h), :] = result.astype(BF16)
                l_out[k - 1, h : h + 1, :] = level
                copies[h].start()
            copies[heads].start()

    @pl.when(z == planes - 1)
    def _():
        last_slot()

    for r in range(1, PLANE):
        @pl.when(places[r] < p)
        def _(r=r):
            for h in range(heads):
                top = score(q_soft[:, cols(h)], h, r)
                merge(h, *finish(h, (r,), top))

    for k in range(planes - 1, 0, -1):
        @pl.when(z >= k)
        def _(k=k):
            for copy in total_copies(k):
                copy.wait_recv()
    ahead = [jnp.where(places[r] < p, spans[r], 0.0) for r in range(PLANE)]
    reach = sum(ahead)
    for k in range(1, planes):
        @pl.when(z >= k)
        def _(k=k):
            gone = reach
            for nearer in range(1, k):
                gone = gone + e_in[nearer - 1]
            for h in range(heads):
                carried[cols(h), :] += jnp.exp(gone[h : h + 1, :]) * t_in[k - 1, cols(h), :].astype(F32)
    for h in range(heads):
        state = carried[cols(h), :]
        high = state.astype(BF16)
        low = (state - high.astype(F32)).astype(BF16)
        query = q_lin[:, cols(h)]
        raw = inside[:, cols(h)] + (dot(query, high) + dot(query, low)) * jnp.exp(sum_col[:, h : h + 1])
        norm = lax.rsqrt(jnp.mean(raw * raw, axis=-1, keepdims=True) + 1e-6)
        gathered[0, group, :, cols(h)] = (raw * norm).astype(BF16)

    def exchange(layer):
        return [
            remote(
                gathered.at[layer, group], gathered.at[layer, group],
                g_ss.at[layer, j], g_rs.at[layer, j], head=lax.rem(group + j, groups),
            )
            for j in range(1, groups)
        ]

    step = min(columns, 512)

    def project_own(layer):
        for c in range(columns // step):
            piece = pl.ds(c * step, step)
            totals[:, piece] = dot(gathered[layer, group], weights[layer, group, :, piece])

    def project_others(layer, out_hbm):
        copies = []
        for c in range(columns // step):
            piece = pl.ds(c * step, step)
            total = totals[:, piece]
            for j in range(1, groups):
                g = lax.rem(group + j, groups)
                total = total + dot(gathered[layer, g], weights[layer, g, :, piece])
            staged[layer, :, piece] = total.astype(BF16)
            copy = pltpu.make_async_copy(
                staged.at[layer, :, piece], out_hbm.at[:, piece], out_ls.at[layer, c]
            )
            copy.start()
            copies.append(copy)
        return copies

    lin_send = exchange(0)
    for copy in lin_send:
        copy.start()
    for copy in own_weights:
        copy.wait()
    project_own(0)
    for copy in weight_send:
        copy.wait_recv()
    for copy in lin_send:
        copy.wait_recv()
    out_copies = project_others(0, lin_hbm)

    for k in range(1, planes):
        @pl.when(z >= k)
        def _(k=k):
            for copy in output_copies(k):
                copy.wait_recv()
            for h in range(heads):
                merge(h, o_in[k - 1, cols(h), :].astype(F32), l_in[k - 1, h : h + 1, :])
    gathered[1, group] = o_self[...].T.astype(BF16)
    soft_send = exchange(1)
    for copy in soft_send:
        copy.start()
    project_own(1)
    for copy in soft_send:
        copy.wait_recv()
    out_copies += project_others(1, soft_hbm)

    for copy in k_send + v_send + [k_pass, v_pass] + weight_send + s_send + d_send + lin_send + soft_send:
        copy.wait_send()
    for k in range(1, planes):
        @pl.when(z >= k)
        def _(k=k):
            query_copy(k).wait_send()

        @pl.when(z + k < planes)
        def _(k=k):
            for copy in list(total_copies(k)) + output_copies(k):
                copy.wait_send()
    for copy in out_copies:
        copy.wait()


def local(planes, groups, *arrays):
    q_lin, _, _, decay, q_soft, _, _, wo_lin, _ = arrays
    rows, both = q_soft.shape
    heads = decay.shape[0]
    width = both // heads
    columns = wo_lin.shape[1] // groups
    far = max(planes - 1, 1)
    near = PLANE - 1
    vmem = pltpu.VMEM
    dma = pltpu.SemaphoreType.DMA
    scratch = [
        vmem((rows, both), BF16),
        vmem((rows, both), BF16),
        vmem((rows, both), BF16),
        vmem(decay.shape, F32),
        vmem((rows, both), BF16),
        vmem((rows, both), BF16),
        vmem((rows, both), BF16),
        vmem((rows, columns), F32),
        vmem((far, rows, both), BF16),
        vmem((near, rows, both), BF16),
        vmem((near, rows, both), BF16),
        vmem((PLANE, both, rows), BF16),
        vmem((heads, PLANE, rows, rows), F32),
        vmem((both, width), BF16),
        vmem((near, both, width), BF16),
        vmem((8, width), F32),
        vmem((near, 8, width), F32),
        vmem((both, width), BF16),
        vmem((far, both, width), BF16),
        vmem((8, width), F32),
        vmem((far, 8, width), F32),
        vmem((both, width), F32),
        vmem((rows, both), F32),
        vmem((far, both, rows), BF16),
        vmem((far, both, rows), BF16),
        vmem((far, 8, rows), F32),
        vmem((far, 8, rows), F32),
        vmem((both, rows), F32),
        vmem((8, rows), F32),
        vmem((2, groups, rows, both), BF16),
        vmem((2, groups, both, columns), BF16),
        vmem((2, rows, columns), BF16),
    ]
    pairs = [(far,)] + [(near,)] * 4 + [(far,)] * 2 + [(far, heads), (far,)]
    for shape in pairs:
        scratch += [dma(shape), dma(shape)]
    for _ in range(2):
        scratch += [dma((2, groups)), dma((2, groups))]
    scratch += [dma((2,)), dma((2, columns // min(columns, 512))), dma((7,))]
    anywhere = pl.BlockSpec(memory_space=pl.ANY)
    out = jax.ShapeDtypeStruct((rows, columns), BF16)
    return pl.pallas_call(
        functools.partial(kernel, planes, groups, heads, 1.0 / math.sqrt(width)),
        out_shape=(out, out),
        in_specs=[anywhere] * 9,
        out_specs=(anywhere, anywhere),
        scratch_shapes=scratch,
        compiler_params=pltpu.CompilerParams(
            collective_id=0, has_side_effects=True, vmem_limit_bytes=60 * 1024 * 1024
        ),
        name="attention_layers",
    )(*arrays)


def solution(mesh):
    planes = mesh.shape["seq"] // PLANE
    groups = mesh.shape["head"]
    in_specs = (P("seq", "head"),) * 3 + (P("head", "seq"),) + (P("seq", "head"),) * 3 + (P("head", None),) * 2
    out_specs = (P("seq", "head"), P("seq", "head"))
    return jax.shard_map(
        functools.partial(local, planes, groups),
        mesh=mesh, in_specs=in_specs, out_specs=out_specs, check_vma=False,
    )
```

```python
import functools
import math

import jax
import jax.numpy as jnp
from jax import lax
from jax.experimental import pallas as pl
from jax.experimental.pallas import tpu as pltpu
from jax.sharding import PartitionSpec as P

HIGHEST = lax.Precision.HIGHEST
MESH = pl.DeviceIdType.MESH
F32 = jnp.float32
BF16 = jnp.bfloat16
PLANE = 4
NEG_BIG = -1e30


def dot(a, b, ca=1, cb=0, precision=None):
    return lax.dot_general(
        a, b, (((ca,), (cb,)), ((), ())), precision=precision, preferred_element_type=F32
    )


def split_dot(a, b):
    high = a.astype(BF16)
    low = (a - high.astype(F32)).astype(BF16)
    return dot(high, b) + dot(low, b)


def kernel(
    planes, groups, heads, factor,
    q_lin_hbm, k_lin_hbm, v_lin_hbm, decay_hbm, q_hbm, k_hbm, v_hbm, wo_lin, wo_soft,
    lin_hbm, soft_hbm,
    q_lin, k_lin, v_lin, decay, q_soft, k_soft, v_soft, totals,
    q_in, k_in, v_in, vt, scores,
    s_own, s_in, d_own, d_in, t_own, t_in, e_own, e_in, carried, inside,
    o_part, o_out, o_in, l_out, l_in, o_self, l_self,
    gathered, weights, staged,
    q_ss, q_rs, k_ss, k_rs, v_ss, v_rs, s_ss, s_rs, d_ss, d_rs,
    t_ss, t_rs, e_ss, e_rs, o_ss, o_rs, l_ss, l_rs, w_ss, w_rs, g_ss, g_rs, w_ls, out_ls, in_ls,
):
    rows = q_soft.shape[0]
    width = q_soft.shape[1] // heads
    columns = weights.shape[3]
    seq = lax.axis_index("seq")
    group = lax.axis_index("head")
    z, p = seq // PLANE, seq % PLANE
    x, y = p % 2, p // 2
    places = (p, 2 * y + 1 - x, 2 * (1 - y) + x, 3 - p)
    chips = tuple(z * PLANE + place for place in places)

    def remote(src, dst, ss, rs, **device):
        return pltpu.make_async_remote_copy(
            src_ref=src, dst_ref=dst, send_sem=ss, recv_sem=rs,
            device_id=device, device_id_type=MESH,
        )

    def cols(h):
        return slice(h * width, (h + 1) * width)

    loads = [
        pltpu.make_async_copy(src, dst, in_ls.at[i])
        for i, (src, dst) in enumerate((
            (decay_hbm, decay), (k_lin_hbm, k_lin), (v_lin_hbm, v_lin), (q_lin_hbm, q_lin),
            (v_hbm, v_soft), (k_hbm, k_soft), (q_hbm, q_soft),
        ))
    ]
    for copy in loads:
        copy.start()

    barrier = pltpu.get_barrier_semaphore()
    for r in range(1, PLANE):
        pl.semaphore_signal(barrier, inc=1, device_id={"seq": chips[r]}, device_id_type=MESH)
    for k in range(1, planes):
        other = lax.rem(z + k, planes) * PLANE + p
        pl.semaphore_signal(barrier, inc=1, device_id={"seq": other}, device_id_type=MESH)
    for j in range(1, groups):
        peer = lax.rem(group + j, groups)
        pl.semaphore_signal(barrier, inc=1, device_id={"head": peer}, device_id_type=MESH)
    own_weights = []
    for layer, wo in enumerate((wo_lin, wo_soft)):
        piece = wo.at[:, pl.ds(pl.multiple_of(group * columns, 128), columns)]
        own_weights.append(
            pltpu.make_async_copy(piece, weights.at[layer, group], w_ls.at[layer])
        )
    for copy in own_weights:
        copy.start()
    pl.semaphore_wait(barrier, PLANE - 1 + planes - 1 + groups - 1)

    k_send = [remote(k_hbm, k_in.at[r - 1], k_ss.at[r - 1], k_rs.at[r - 1], seq=chips[r]) for r in (1, 2)]
    v_send = [remote(v_hbm, v_in.at[r - 1], v_ss.at[r - 1], v_rs.at[r - 1], seq=chips[r]) for r in (1, 2)]
    k_send[0].start()
    v_send[1].start()
    v_send[0].start()
    k_send[1].start()

    def query_copy(k):
        return remote(
            q_hbm, q_in.at[k - 1], q_ss.at[k - 1], q_rs.at[k - 1], seq=(z - k) * PLANE + p
        )

    for k in range(planes - 1, 0, -1):
        @pl.when(z >= k)
        def _(k=k):
            query_copy(k).start()

    weight_send = []
    for layer, wo in enumerate((wo_lin, wo_soft)):
        for j in range(1, groups):
            peer = lax.rem(group + j, groups)
            piece = wo.at[:, pl.ds(pl.multiple_of(peer * columns, 128), columns)]
            weight_send.append(
                remote(piece, weights.at[layer, group], w_ss.at[layer, j], w_rs.at[layer, j], head=peer)
            )
    for copy in weight_send:
        copy.start()

    before = lax.broadcasted_iota(jnp.int32, (rows, rows), 1)
    after = lax.broadcasted_iota(jnp.int32, (rows, rows), 0)
    lower = before <= after
    for copy in loads[:3]:
        copy.wait()
    triangle = lower.astype(F32)
    sum_row = dot(decay[...], triangle, 1, 1, HIGHEST)
    sum_col = dot(triangle, decay[...], 1, 1, HIGHEST)
    d_own[...] = jnp.zeros_like(d_own)
    for h in range(heads):
        row = sum_row[h : h + 1, :]
        total = row[:, rows - 1 : rows]
        d_own[h : h + 1, :] = jnp.broadcast_to(total, (1, width))
        faded = k_lin[:, cols(h)].astype(F32).T * jnp.exp(total - row)
        s_own[cols(h), :] = split_dot(faded, v_lin[:, cols(h)]).astype(BF16)
    s_send = [
        remote(s_own, s_in.at[r - 1], s_ss.at[r - 1], s_rs.at[r - 1], seq=chips[r])
        for r in range(1, PLANE)
    ]
    d_send = [
        remote(d_own, d_in.at[r - 1], d_ss.at[r - 1], d_rs.at[r - 1], seq=chips[r])
        for r in range(1, PLANE)
    ]
    for copy in s_send + d_send:
        copy.start()

    for copy in loads[3:]:
        copy.wait()
    for h in range(heads):
        gap = jnp.where(lower, sum_col[:, h : h + 1] - sum_row[h : h + 1, :], NEG_BIG)
        near = dot(q_lin[:, cols(h)], k_lin[:, cols(h)], 1, 1) * jnp.exp(gap)
        inside[:, cols(h)] = split_dot(near, v_lin[:, cols(h)])
    vt[0] = v_soft[...].T

    for copy in s_send + d_send:
        copy.wait_recv()
    spans = [d_own[...]] + [d_in[r] for r in range(PLANE - 1)]
    e_own[...] = sum(spans)
    for h in range(heads):
        whole = jnp.zeros((width, width), F32)
        earlier = jnp.zeros((width, width), F32)
        for r in range(PLANE):
            state = (s_own if r == 0 else s_in.at[r - 1])[cols(h), :].astype(F32)
            to_end = jnp.zeros((1, width), F32)
            to_here = jnp.zeros((1, width), F32)
            for other in range(PLANE):
                span = spans[other][h : h + 1, :]
                later = places[other] > places[r]
                to_end = to_end + jnp.where(later, span, 0.0)
                to_here = to_here + jnp.where(later & (places[other] < p), span, 0.0)
            whole = whole + jnp.exp(to_end) * state
            earlier = earlier + jnp.where(places[r] < p, jnp.exp(to_here), 0.0) * state
        t_own[cols(h), :] = whole.astype(BF16)
        carried[cols(h), :] = earlier

    def total_copies(k):
        there = (z + k) * PLANE + p
        return (
            remote(t_own, t_in.at[k - 1], t_ss.at[k - 1], t_rs.at[k - 1], seq=there),
            remote(e_own, e_in.at[k - 1], e_ss.at[k - 1], e_rs.at[k - 1], seq=there),
        )

    for k in range(1, planes):
        @pl.when(z + k < planes)
        def _(k=k):
            for copy in total_copies(k):
                copy.start()

    k_send[0].wait_recv()
    k_pass = remote(k_in.at[0], k_in.at[2], k_ss.at[2], k_rs.at[2], seq=chips[2])
    k_pass.start()
    v_send[1].wait_recv()
    v_pass = remote(v_in.at[1], v_in.at[2], v_ss.at[2], v_rs.at[2], seq=chips[1])
    v_pass.start()

    scale = factor * math.log2(math.e)

    def score(query, h, r, top=None, masked=False):
        keys = (k_soft if r == 0 else k_in.at[r - 1])[:, cols(h)]
        part = dot(keys, query, 1, 1)
        if masked:
            part = jnp.where(after <= before, part, NEG_BIG)
        scores[h, r] = part
        best = jnp.max(part, axis=0, keepdims=True)
        return best if top is None else jnp.maximum(top, best)

    def finish(h, slots, top):
        total = jnp.zeros_like(top)
        result = jnp.zeros((width, rows), F32)
        for r in slots:
            weight = jnp.exp2((scores[h, r] - top) * scale)
            total = total + jnp.sum(weight, axis=0, keepdims=True)
            result = result + dot(vt[r, cols(h), :], weight.astype(BF16))
        return result / total, top * scale + jnp.log2(total)

    def merged(mine, level_here, theirs, level_there):
        level = jnp.maximum(level_here, level_there)
        a, b = jnp.exp2(level_here - level), jnp.exp2(level_there - level)
        both = a + b
        return mine * (a / both) + theirs * (b / both), level + jnp.log2(both)

    def merge(h, theirs, level_there):
        o_self[cols(h), :], l_self[h : h + 1, :] = merged(
            o_self[cols(h), :], l_self[h : h + 1, :], theirs, level_there
        )

    for h in range(heads):
        top = score(q_soft[:, cols(h)], h, 0, masked=True)
        o_self[cols(h), :], l_self[h : h + 1, :] = finish(h, (0,), top)
    vt[2] = v_in[1].T
    v_send[0].wait_recv()
    vt[1] = v_in[0].T
    k_send[1].wait_recv()

    def last_slot():
        k_pass.wait_recv()
        v_pass.wait_recv()
        vt[3] = v_in[2].T

    def output_copies(k, h):
        there = (z + 1) * PLANE + p
        return (
            remote(
                o_out.at[k - 1, cols(h)], o_in.at[k - 1, cols(h)],
                o_ss.at[k - 1, h], o_rs.at[k - 1, h], seq=there,
            ),
            remote(
                l_out.at[k - 1, h], l_in.at[k - 1, h],
                l_ss.at[k - 1, h], l_rs.at[k - 1, h], seq=there,
            ),
        )

    for target in range(planes - 1, 0, -1):
        @pl.when(z < target)
        def _(target=target):
            k = target - z
            query_copy(k).wait_recv()
            queries = [q_in[k - 1, :, cols(h)] for h in range(heads)]
            tops = [None] * heads
            for h in range(heads):
                for r in range(PLANE - 1):
                    tops[h] = score(queries[h], h, r, tops[h])
            if target == planes - 1:
                last_slot()
            for h in range(heads):
                tops[h] = score(queries[h], h, PLANE - 1, tops[h])
                result, level = finish(h, range(PLANE), tops[h])
                o_part[k - 1, cols(h), :] = result
                l_out[k - 1, h] = jnp.broadcast_to(level, (8, rows))

                @pl.when(z == 0)
                def _(h=h, k=k):
                    o_out[k - 1, cols(h), :] = o_part[k - 1, cols(h), :].astype(BF16)
                    for copy in output_copies(k, h):
                        copy.start()

    @pl.when(z == planes - 1)
    def _():
        last_slot()

    def own_rows(chosen):
        for r in range(1, PLANE):
            @pl.when(chosen & (places[r] < p))
            def _(r=r):
                for h in range(heads):
                    top = score(q_soft[:, cols(h)], h, r)
                    merge(h, *finish(h, (r,), top))

    own_rows(z >= 2)

    for target in range(planes - 1, 1, -1):
        @pl.when((z >= 1) & (z < target))
        def _(target=target):
            k = target - z
            for h in range(heads):
                for copy in output_copies(k + 1, h):
                    copy.wait_recv()
                result, level = merged(
                    o_part[k - 1, cols(h), :], l_out[k - 1, h, 0:1, :],
                    o_in[k, cols(h), :].astype(F32), l_in[k, h, 0:1, :],
                )
                o_out[k - 1, cols(h), :] = result.astype(BF16)
                l_out[k - 1, h] = jnp.broadcast_to(level, (8, rows))
                for copy in output_copies(k, h):
                    copy.start()

    own_rows(z < 2)

    for k in range(planes - 1, 0, -1):
        @pl.when(z >= k)
        def _(k=k):
            for copy in total_copies(k):
                copy.wait_recv()
    ahead = [jnp.where(places[r] < p, spans[r], 0.0) for r in range(PLANE)]
    reach = sum(ahead)
    for k in range(1, planes):
        @pl.when(z >= k)
        def _(k=k):
            gone = reach
            for nearer in range(1, k):
                gone = gone + e_in[nearer - 1]
            for h in range(heads):
                carried[cols(h), :] += jnp.exp(gone[h : h + 1, :]) * t_in[k - 1, cols(h), :].astype(F32)
    for h in range(heads):
        state = carried[cols(h), :]
        high = state.astype(BF16)
        low = (state - high.astype(F32)).astype(BF16)
        query = q_lin[:, cols(h)]
        raw = inside[:, cols(h)] + (dot(query, high) + dot(query, low)) * jnp.exp(sum_col[:, h : h + 1])
        norm = lax.rsqrt(jnp.mean(raw * raw, axis=-1, keepdims=True) + 1e-6)
        gathered[0, group, :, cols(h)] = (raw * norm).astype(BF16)

    def exchange(layer):
        return [
            remote(
                gathered.at[layer, group], gathered.at[layer, group],
                g_ss.at[layer, j], g_rs.at[layer, j], head=lax.rem(group + j, groups),
            )
            for j in range(1, groups)
        ]

    step = min(columns, 512)

    def project_own(layer):
        for c in range(columns // step):
            piece = pl.ds(c * step, step)
            totals[:, piece] = dot(gathered[layer, group], weights[layer, group, :, piece])

    def project_others(layer, out_hbm):
        copies = []
        for c in range(columns // step):
            piece = pl.ds(c * step, step)
            total = totals[:, piece]
            for j in range(1, groups):
                g = lax.rem(group + j, groups)
                total = total + dot(gathered[layer, g], weights[layer, g, :, piece])
            staged[layer, :, piece] = total.astype(BF16)
            copy = pltpu.make_async_copy(
                staged.at[layer, :, piece], out_hbm.at[:, piece], out_ls.at[layer, c]
            )
            copy.start()
            copies.append(copy)
        return copies

    lin_send = exchange(0)
    for copy in lin_send:
        copy.start()
    for copy in own_weights:
        copy.wait()
    project_own(0)
    for copy in weight_send:
        copy.wait_recv()
    for copy in lin_send:
        copy.wait_recv()
    out_copies = project_others(0, lin_hbm)

    @pl.when(z >= 1)
    def _():
        for h in range(heads):
            for copy in output_copies(1, h):
                copy.wait_recv()
            merge(h, o_in[0, cols(h), :].astype(F32), l_in[0, h, 0:1, :])

    gathered[1, group] = o_self[...].T.astype(BF16)
    soft_send = exchange(1)
    for copy in soft_send:
        copy.start()
    project_own(1)
    for copy in soft_send:
        copy.wait_recv()
    out_copies += project_others(1, soft_hbm)

    for copy in k_send + v_send + [k_pass, v_pass] + weight_send + s_send + d_send + lin_send + soft_send:
        copy.wait_send()
    for k in range(1, planes):
        @pl.when(z >= k)
        def _(k=k):
            query_copy(k).wait_send()

        @pl.when(z + k < planes)
        def _(k=k):
            for copy in total_copies(k):
                copy.wait_send()
            for h in range(heads):
                for copy in output_copies(k, h):
                    copy.wait_send()
    for copy in out_copies:
        copy.wait()


def local(planes, groups, *arrays):
    q_lin, _, _, decay, q_soft, _, _, wo_lin, _ = arrays
    rows, both = q_soft.shape
    heads = decay.shape[0]
    width = both // heads
    columns = wo_lin.shape[1] // groups
    far = max(planes - 1, 1)
    near = PLANE - 1
    vmem = pltpu.VMEM
    dma = pltpu.SemaphoreType.DMA
    scratch = [
        vmem((rows, both), BF16),
        vmem((rows, both), BF16),
        vmem((rows, both), BF16),
        vmem(decay.shape, F32),
        vmem((rows, both), BF16),
        vmem((rows, both), BF16),
        vmem((rows, both), BF16),
        vmem((rows, columns), F32),
        vmem((far, rows, both), BF16),
        vmem((near, rows, both), BF16),
        vmem((near, rows, both), BF16),
        vmem((PLANE, both, rows), BF16),
        vmem((heads, PLANE, rows, rows), F32),
        vmem((both, width), BF16),
        vmem((near, both, width), BF16),
        vmem((8, width), F32),
        vmem((near, 8, width), F32),
        vmem((both, width), BF16),
        vmem((far, both, width), BF16),
        vmem((8, width), F32),
        vmem((far, 8, width), F32),
        vmem((both, width), F32),
        vmem((rows, both), F32),
        vmem((far, both, rows), F32),
        vmem((far, both, rows), BF16),
        vmem((far, both, rows), BF16),
        vmem((far, heads, 8, rows), F32),
        vmem((far, heads, 8, rows), F32),
        vmem((both, rows), F32),
        vmem((8, rows), F32),
        vmem((2, groups, rows, both), BF16),
        vmem((2, groups, both, columns), BF16),
        vmem((2, rows, columns), BF16),
    ]
    pairs = [(far,)] + [(near,)] * 4 + [(far,)] * 2 + [(far, heads)] * 2
    for shape in pairs:
        scratch += [dma(shape), dma(shape)]
    for _ in range(2):
        scratch += [dma((2, groups)), dma((2, groups))]
    scratch += [dma((2,)), dma((2, columns // min(columns, 512))), dma((7,))]
    anywhere = pl.BlockSpec(memory_space=pl.ANY)
    out = jax.ShapeDtypeStruct((rows, columns), BF16)
    return pl.pallas_call(
        functools.partial(kernel, planes, groups, heads, 1.0 / math.sqrt(width)),
        out_shape=(out, out),
        in_specs=[anywhere] * 9,
        out_specs=(anywhere, anywhere),
        scratch_shapes=scratch,
        compiler_params=pltpu.CompilerParams(
            collective_id=0, has_side_effects=True, vmem_limit_bytes=60 * 1024 * 1024
        ),
        name="attention_layers",
    )(*arrays)


def solution(mesh):
    planes = mesh.shape["seq"] // PLANE
    groups = mesh.shape["head"]
    in_specs = (P("seq", "head"),) * 3 + (P("head", "seq"),) + (P("seq", "head"),) * 3 + (P("head", None),) * 2
    out_specs = (P("seq", "head"), P("seq", "head"))
    return jax.shard_map(
        functools.partial(local, planes, groups),
        mesh=mesh, in_specs=in_specs, out_specs=out_specs, check_vma=False,
    )
```

```python
import functools
import math

import jax
import jax.numpy as jnp
from jax import lax
from jax.experimental import pallas as pl
from jax.experimental.pallas import tpu as pltpu
from jax.sharding import PartitionSpec as P

HIGHEST = lax.Precision.HIGHEST
MESH = pl.DeviceIdType.MESH
F32 = jnp.float32
BF16 = jnp.bfloat16
PLANE = 4
NEG_BIG = -1e30


def dot(a, b, ca=1, cb=0, precision=None):
    return lax.dot_general(
        a, b, (((ca,), (cb,)), ((), ())), precision=precision, preferred_element_type=F32
    )


def split_dot(a, b):
    high = a.astype(BF16)
    low = (a - high.astype(F32)).astype(BF16)
    return dot(high, b) + dot(low, b)


def kernel(
    planes, groups, heads, factor,
    q_lin_hbm, k_lin_hbm, v_lin_hbm, decay_hbm, q_hbm, k_hbm, v_hbm, wo_lin, wo_soft,
    lin_hbm, soft_hbm,
    q_lin, k_lin, v_lin, decay, q_soft, k_soft, v_soft, totals,
    q_in, k_in, v_in, vt, scores,
    s_own, s_in, d_own, d_in, t_own, t_in, e_own, e_in, carried, inside,
    o_part, o_out, o_in, l_out, l_in, o_self, l_self,
    gathered, weights, staged,
    q_ss, q_rs, k_ss, k_rs, v_ss, v_rs, s_ss, s_rs, d_ss, d_rs,
    t_ss, t_rs, e_ss, e_rs, o_ss, o_rs, l_ss, l_rs, w_ss, w_rs, g_ss, g_rs, w_ls, out_ls, in_ls,
):
    rows = q_soft.shape[0]
    width = q_soft.shape[1] // heads
    columns = weights.shape[3]
    seq = lax.axis_index("seq")
    group = lax.axis_index("head")
    z, p = seq // PLANE, seq % PLANE
    x, y = p % 2, p // 2
    places = (p, 2 * y + 1 - x, 2 * (1 - y) + x, 3 - p)
    chips = tuple(z * PLANE + place for place in places)

    def remote(src, dst, ss, rs, **device):
        return pltpu.make_async_remote_copy(
            src_ref=src, dst_ref=dst, send_sem=ss, recv_sem=rs,
            device_id=device, device_id_type=MESH,
        )

    def cols(h):
        return slice(h * width, (h + 1) * width)

    loads = [
        pltpu.make_async_copy(src, dst, in_ls.at[i])
        for i, (src, dst) in enumerate((
            (decay_hbm, decay), (k_lin_hbm, k_lin), (v_lin_hbm, v_lin), (q_lin_hbm, q_lin),
            (v_hbm, v_soft), (k_hbm, k_soft), (q_hbm, q_soft),
        ))
    ]
    for copy in loads:
        copy.start()

    barrier = pltpu.get_barrier_semaphore()
    for r in range(1, PLANE):
        pl.semaphore_signal(barrier, inc=1, device_id={"seq": chips[r]}, device_id_type=MESH)
    for k in range(1, planes):
        other = lax.rem(z + k, planes) * PLANE + p
        pl.semaphore_signal(barrier, inc=1, device_id={"seq": other}, device_id_type=MESH)
    for j in range(1, groups):
        peer = lax.rem(group + j, groups)
        pl.semaphore_signal(barrier, inc=1, device_id={"head": peer}, device_id_type=MESH)
    own_weights = []
    for layer, wo in enumerate((wo_lin, wo_soft)):
        piece = wo.at[:, pl.ds(pl.multiple_of(group * columns, 128), columns)]
        own_weights.append(
            pltpu.make_async_copy(piece, weights.at[layer, group], w_ls.at[layer])
        )
    for copy in own_weights:
        copy.start()
    pl.semaphore_wait(barrier, PLANE - 1 + planes - 1 + groups - 1)

    k_send = [remote(k_hbm, k_in.at[r - 1], k_ss.at[r - 1], k_rs.at[r - 1], seq=chips[r]) for r in (1, 2)]
    v_send = [remote(v_hbm, v_in.at[r - 1], v_ss.at[r - 1], v_rs.at[r - 1], seq=chips[r]) for r in (1, 2)]
    k_send[0].start()
    v_send[1].start()
    v_send[0].start()
    k_send[1].start()

    def query_copy(k):
        return remote(
            q_hbm, q_in.at[k - 1], q_ss.at[k - 1], q_rs.at[k - 1], seq=(z - k) * PLANE + p
        )

    for k in range(planes - 1, 0, -1):
        @pl.when(z >= k)
        def _(k=k):
            query_copy(k).start()

    weight_send = []
    for layer, wo in enumerate((wo_lin, wo_soft)):
        for j in range(1, groups):
            peer = lax.rem(group + j, groups)
            piece = wo.at[:, pl.ds(pl.multiple_of(peer * columns, 128), columns)]
            weight_send.append(
                remote(piece, weights.at[layer, group], w_ss.at[layer, j], w_rs.at[layer, j], head=peer)
            )
    for copy in weight_send:
        copy.start()

    before = lax.broadcasted_iota(jnp.int32, (rows, rows), 1)
    after = lax.broadcasted_iota(jnp.int32, (rows, rows), 0)
    lower = before <= after
    for copy in loads[:3]:
        copy.wait()
    triangle = lower.astype(F32)
    sum_row = dot(decay[...], triangle, 1, 1, HIGHEST)
    sum_col = dot(triangle, decay[...], 1, 1, HIGHEST)
    d_own[...] = jnp.zeros_like(d_own)
    for h in range(heads):
        row = sum_row[h : h + 1, :]
        total = row[:, rows - 1 : rows]
        d_own[h : h + 1, :] = jnp.broadcast_to(total, (1, width))
        faded = k_lin[:, cols(h)].astype(F32).T * jnp.exp(total - row)
        s_own[cols(h), :] = split_dot(faded, v_lin[:, cols(h)]).astype(BF16)
    s_send = [
        remote(s_own, s_in.at[r - 1], s_ss.at[r - 1], s_rs.at[r - 1], seq=chips[r])
        for r in range(1, PLANE)
    ]
    d_send = [
        remote(d_own, d_in.at[r - 1], d_ss.at[r - 1], d_rs.at[r - 1], seq=chips[r])
        for r in range(1, PLANE)
    ]
    for copy in s_send + d_send:
        copy.start()

    for copy in loads[3:]:
        copy.wait()
    for h in range(heads):
        gap = jnp.where(lower, sum_col[:, h : h + 1] - sum_row[h : h + 1, :], NEG_BIG)
        near = dot(q_lin[:, cols(h)], k_lin[:, cols(h)], 1, 1) * jnp.exp(gap)
        inside[:, cols(h)] = split_dot(near, v_lin[:, cols(h)])
    vt[0] = v_soft[...].T

    k_send[0].wait_recv()
    k_pass = remote(k_in.at[0], k_in.at[2], k_ss.at[2], k_rs.at[2], seq=chips[2])
    k_pass.start()
    v_send[1].wait_recv()
    v_pass = remote(v_in.at[1], v_in.at[2], v_ss.at[2], v_rs.at[2], seq=chips[1])
    v_pass.start()

    for copy in s_send + d_send:
        copy.wait_recv()
    spans = [d_own[...]] + [d_in[r] for r in range(PLANE - 1)]
    e_own[...] = sum(spans)
    for h in range(heads):
        whole = jnp.zeros((width, width), F32)
        earlier = jnp.zeros((width, width), F32)
        for r in range(PLANE):
            state = (s_own if r == 0 else s_in.at[r - 1])[cols(h), :].astype(F32)
            to_end = jnp.zeros((1, width), F32)
            to_here = jnp.zeros((1, width), F32)
            for other in range(PLANE):
                span = spans[other][h : h + 1, :]
                later = places[other] > places[r]
                to_end = to_end + jnp.where(later, span, 0.0)
                to_here = to_here + jnp.where(later & (places[other] < p), span, 0.0)
            whole = whole + jnp.exp(to_end) * state
            earlier = earlier + jnp.where(places[r] < p, jnp.exp(to_here), 0.0) * state
        t_own[cols(h), :] = whole.astype(BF16)
        carried[cols(h), :] = earlier

    def total_copies(k):
        there = (z + k) * PLANE + p
        return (
            remote(t_own, t_in.at[k - 1], t_ss.at[k - 1], t_rs.at[k - 1], seq=there),
            remote(e_own, e_in.at[k - 1], e_ss.at[k - 1], e_rs.at[k - 1], seq=there),
        )

    for k in range(1, planes):
        @pl.when(z + k < planes)
        def _(k=k):
            for copy in total_copies(k):
                copy.start()

    scale = factor * math.log2(math.e)

    def score(query, h, r, top=None, masked=False):
        keys = (k_soft if r == 0 else k_in.at[r - 1])[:, cols(h)]
        part = dot(keys, query, 1, 1)
        if masked:
            part = jnp.where(after <= before, part, NEG_BIG)
        scores[h, r] = part
        best = jnp.max(part, axis=0, keepdims=True)
        return best if top is None else jnp.maximum(top, best)

    def finish(h, slots, top):
        total = jnp.zeros_like(top)
        result = jnp.zeros((width, rows), F32)
        for r in slots:
            weight = jnp.exp2((scores[h, r] - top) * scale)
            total = total + jnp.sum(weight, axis=0, keepdims=True)
            result = result + dot(vt[r, cols(h), :], weight.astype(BF16))
        return result / total, top * scale + jnp.log2(total)

    def merged(mine, level_here, theirs, level_there):
        level = jnp.maximum(level_here, level_there)
        a, b = jnp.exp2(level_here - level), jnp.exp2(level_there - level)
        both = a + b
        return mine * (a / both) + theirs * (b / both), level + jnp.log2(both)

    def merge(h, theirs, level_there):
        o_self[cols(h), :], l_self[h : h + 1, :] = merged(
            o_self[cols(h), :], l_self[h : h + 1, :], theirs, level_there
        )

    for h in range(heads):
        top = score(q_soft[:, cols(h)], h, 0, masked=True)
        o_self[cols(h), :], l_self[h : h + 1, :] = finish(h, (0,), top)
    vt[2] = v_in[1].T
    v_send[0].wait_recv()
    vt[1] = v_in[0].T
    k_send[1].wait_recv()

    def last_slot():
        k_pass.wait_recv()
        v_pass.wait_recv()
        vt[3] = v_in[2].T

    def output_copies(k, h):
        there = (z + 1) * PLANE + p
        return (
            remote(
                o_out.at[k - 1, cols(h)], o_in.at[k - 1, cols(h)],
                o_ss.at[k - 1, h], o_rs.at[k - 1, h], seq=there,
            ),
            remote(
                l_out.at[k - 1, h], l_in.at[k - 1, h],
                l_ss.at[k - 1, h], l_rs.at[k - 1, h], seq=there,
            ),
        )

    for target in range(planes - 1, 0, -1):
        @pl.when(z < target)
        def _(target=target):
            k = target - z
            query_copy(k).wait_recv()
            queries = [q_in[k - 1, :, cols(h)] for h in range(heads)]
            tops = [None] * heads
            for h in range(heads):
                for r in range(PLANE - 1):
                    tops[h] = score(queries[h], h, r, tops[h])
            if target == planes - 1:
                last_slot()
            for h in range(heads):
                tops[h] = score(queries[h], h, PLANE - 1, tops[h])
                result, level = finish(h, range(PLANE), tops[h])
                o_part[k - 1, cols(h), :] = result
                l_out[k - 1, h] = jnp.broadcast_to(level, (8, rows))

                @pl.when(z == 0)
                def _(h=h, k=k):
                    o_out[k - 1, cols(h), :] = o_part[k - 1, cols(h), :].astype(BF16)
                    for copy in output_copies(k, h):
                        copy.start()

    @pl.when(z == planes - 1)
    def _():
        last_slot()

    def own_rows(chosen):
        for r in range(1, PLANE):
            @pl.when(chosen & (places[r] < p))
            def _(r=r):
                for h in range(heads):
                    top = score(q_soft[:, cols(h)], h, r)
                    merge(h, *finish(h, (r,), top))

    own_rows(z >= 2)

    for target in range(planes - 1, 1, -1):
        @pl.when((z >= 1) & (z < target))
        def _(target=target):
            k = target - z
            for h in range(heads):
                for copy in output_copies(k + 1, h):
                    copy.wait_recv()
                result, level = merged(
                    o_part[k - 1, cols(h), :], l_out[k - 1, h, 0:1, :],
                    o_in[k, cols(h), :].astype(F32), l_in[k, h, 0:1, :],
                )
                o_out[k - 1, cols(h), :] = result.astype(BF16)
                l_out[k - 1, h] = jnp.broadcast_to(level, (8, rows))
                for copy in output_copies(k, h):
                    copy.start()

    own_rows(z < 2)

    for k in range(planes - 1, 0, -1):
        @pl.when(z >= k)
        def _(k=k):
            for copy in total_copies(k):
                copy.wait_recv()
    ahead = [jnp.where(places[r] < p, spans[r], 0.0) for r in range(PLANE)]
    reach = sum(ahead)
    for k in range(1, planes):
        @pl.when(z >= k)
        def _(k=k):
            gone = reach
            for nearer in range(1, k):
                gone = gone + e_in[nearer - 1]
            for h in range(heads):
                carried[cols(h), :] += jnp.exp(gone[h : h + 1, :]) * t_in[k - 1, cols(h), :].astype(F32)
    for h in range(heads):
        state = carried[cols(h), :]
        high = state.astype(BF16)
        low = (state - high.astype(F32)).astype(BF16)
        query = q_lin[:, cols(h)]
        raw = inside[:, cols(h)] + (dot(query, high) + dot(query, low)) * jnp.exp(sum_col[:, h : h + 1])
        norm = lax.rsqrt(jnp.mean(raw * raw, axis=-1, keepdims=True) + 1e-6)
        gathered[0, group, :, cols(h)] = (raw * norm).astype(BF16)

    def exchange(layer):
        return [
            remote(
                gathered.at[layer, group], gathered.at[layer, group],
                g_ss.at[layer, j], g_rs.at[layer, j], head=lax.rem(group + j, groups),
            )
            for j in range(1, groups)
        ]

    step = min(columns, 512)

    def project_own(layer):
        for c in range(columns // step):
            piece = pl.ds(c * step, step)
            totals[:, piece] = dot(gathered[layer, group], weights[layer, group, :, piece])

    def project_others(layer, out_hbm):
        copies = []
        for c in range(columns // step):
            piece = pl.ds(c * step, step)
            total = totals[:, piece]
            for j in range(1, groups):
                g = lax.rem(group + j, groups)
                total = total + dot(gathered[layer, g], weights[layer, g, :, piece])
            staged[layer, :, piece] = total.astype(BF16)
            copy = pltpu.make_async_copy(
                staged.at[layer, :, piece], out_hbm.at[:, piece], out_ls.at[layer, c]
            )
            copy.start()
            copies.append(copy)
        return copies

    lin_send = exchange(0)
    for copy in lin_send:
        copy.start()
    for copy in own_weights:
        copy.wait()
    project_own(0)
    for copy in weight_send:
        copy.wait_recv()
    for copy in lin_send:
        copy.wait_recv()
    out_copies = project_others(0, lin_hbm)

    @pl.when(z >= 1)
    def _():
        for h in range(heads):
            for copy in output_copies(1, h):
                copy.wait_recv()
            merge(h, o_in[0, cols(h), :].astype(F32), l_in[0, h, 0:1, :])

    gathered[1, group] = o_self[...].T.astype(BF16)
    soft_send = exchange(1)
    for copy in soft_send:
        copy.start()
    project_own(1)
    for copy in soft_send:
        copy.wait_recv()
    out_copies += project_others(1, soft_hbm)

    for copy in k_send + v_send + [k_pass, v_pass] + weight_send + s_send + d_send + lin_send + soft_send:
        copy.wait_send()
    for k in range(1, planes):
        @pl.when(z >= k)
        def _(k=k):
            query_copy(k).wait_send()

        @pl.when(z + k < planes)
        def _(k=k):
            for copy in total_copies(k):
                copy.wait_send()
            for h in range(heads):
                for copy in output_copies(k, h):
                    copy.wait_send()
    for copy in out_copies:
        copy.wait()


def deliver_kernel(lin, soft, lin_out, soft_out, held, in_sem, out_sem):
    chunks = held.shape[1]
    rows = held.shape[2]
    fetch, store = [], []
    for layer, (src, dst) in enumerate(((lin, lin_out), (soft, soft_out))):
        for c in range(chunks):
            piece = pl.ds(c * rows, rows)
            fetch.append(
                pltpu.make_async_copy(src.at[piece], held.at[layer, c], in_sem.at[layer, c])
            )
            store.append(
                pltpu.make_async_copy(held.at[layer, c], dst.at[piece], out_sem.at[layer, c])
            )
    for copy in fetch:
        copy.start()
    for arrived, copy in zip(fetch, store):
        arrived.wait()
        copy.start()
    for copy in store:
        copy.wait()


def deliver(lin, soft):
    rows, columns = lin.shape
    chunks = 4
    anywhere = pl.BlockSpec(memory_space=pl.ANY)
    out = jax.ShapeDtypeStruct(lin.shape, lin.dtype)
    return pl.pallas_call(
        deliver_kernel,
        out_shape=(out, out),
        in_specs=[anywhere] * 2,
        out_specs=(anywhere, anywhere),
        scratch_shapes=[
            pltpu.VMEM((2, chunks, rows // chunks, columns), BF16),
            pltpu.SemaphoreType.DMA((2, chunks)),
            pltpu.SemaphoreType.DMA((2, chunks)),
        ],
        compiler_params=pltpu.CompilerParams(vmem_limit_bytes=60 * 1024 * 1024),
        name="deliver",
    )(lin, soft)


def local(planes, groups, *arrays):
    q_lin, _, _, decay, q_soft, _, _, wo_lin, _ = arrays
    rows, both = q_soft.shape
    heads = decay.shape[0]
    width = both // heads
    columns = wo_lin.shape[1] // groups
    far = max(planes - 1, 1)
    near = PLANE - 1
    vmem = pltpu.VMEM
    dma = pltpu.SemaphoreType.DMA
    scratch = [
        vmem((rows, both), BF16),
        vmem((rows, both), BF16),
        vmem((rows, both), BF16),
        vmem(decay.shape, F32),
        vmem((rows, both), BF16),
        vmem((rows, both), BF16),
        vmem((rows, both), BF16),
        vmem((rows, columns), F32),
        vmem((far, rows, both), BF16),
        vmem((near, rows, both), BF16),
        vmem((near, rows, both), BF16),
        vmem((PLANE, both, rows), BF16),
        vmem((heads, PLANE, rows, rows), F32),
        vmem((both, width), BF16),
        vmem((near, both, width), BF16),
        vmem((8, width), F32),
        vmem((near, 8, width), F32),
        vmem((both, width), BF16),
        vmem((far, both, width), BF16),
        vmem((8, width), F32),
        vmem((far, 8, width), F32),
        vmem((both, width), F32),
        vmem((rows, both), F32),
        vmem((far, both, rows), F32),
        vmem((far, both, rows), BF16),
        vmem((far, both, rows), BF16),
        vmem((far, heads, 8, rows), F32),
        vmem((far, heads, 8, rows), F32),
        vmem((both, rows), F32),
        vmem((8, rows), F32),
        vmem((2, groups, rows, both), BF16),
        vmem((2, groups, both, columns), BF16),
        vmem((2, rows, columns), BF16),
    ]
    pairs = [(far,)] + [(near,)] * 4 + [(far,)] * 2 + [(far, heads)] * 2
    for shape in pairs:
        scratch += [dma(shape), dma(shape)]
    for _ in range(2):
        scratch += [dma((2, groups)), dma((2, groups))]
    scratch += [dma((2,)), dma((2, columns // min(columns, 512))), dma((7,))]
    anywhere = pl.BlockSpec(memory_space=pl.ANY)
    out = jax.ShapeDtypeStruct((rows, columns), BF16)
    results = pl.pallas_call(
        functools.partial(kernel, planes, groups, heads, 1.0 / math.sqrt(width)),
        out_shape=(out, out),
        in_specs=[anywhere] * 9,
        out_specs=(anywhere, anywhere),
        scratch_shapes=scratch,
        compiler_params=pltpu.CompilerParams(
            collective_id=0, has_side_effects=True, vmem_limit_bytes=60 * 1024 * 1024
        ),
        name="attention_layers",
    )(*arrays)
    return deliver(*results)


def solution(mesh):
    planes = mesh.shape["seq"] // PLANE
    groups = mesh.shape["head"]
    in_specs = (P("seq", "head"),) * 3 + (P("head", "seq"),) + (P("seq", "head"),) * 3 + (P("head", None),) * 2
    out_specs = (P("seq", "head"), P("seq", "head"))
    return jax.shard_map(
        functools.partial(local, planes, groups),
        mesh=mesh, in_specs=in_specs, out_specs=out_specs, check_vma=False,
    )
```

```python
import functools
import math

import jax
import jax.numpy as jnp
from jax import lax
from jax.experimental import pallas as pl
from jax.experimental.pallas import tpu as pltpu
from jax.sharding import PartitionSpec as P

HIGHEST = lax.Precision.HIGHEST
MESH = pl.DeviceIdType.MESH
F32 = jnp.float32
BF16 = jnp.bfloat16
PLANE = 4
NEG_BIG = -1e30


def dot(a, b, ca=1, cb=0, precision=None):
    return lax.dot_general(
        a, b, (((ca,), (cb,)), ((), ())), precision=precision, preferred_element_type=F32
    )


def split_dot(a, b):
    high = a.astype(BF16)
    low = (a - high.astype(F32)).astype(BF16)
    return dot(high, b) + dot(low, b)


def kernel(
    planes, groups, heads, factor,
    q_lin_hbm, k_lin_hbm, v_lin_hbm, decay_hbm, q_hbm, k_hbm, v_hbm, wo_lin, wo_soft,
    lin_hbm, soft_hbm,
    q_lin, k_lin, v_lin, decay, q_soft, k_soft, v_soft, totals,
    q_in, k_in, v_in, vt, scores,
    s_own, s_in, d_own, d_in, t_own, t_in, e_own, e_in, carried, inside,
    o_part, o_out, o_in, l_out, l_in, o_self, l_self,
    gathered, weights, staged,
    q_ss, q_rs, k_ss, k_rs, v_ss, v_rs, s_ss, s_rs, d_ss, d_rs,
    t_ss, t_rs, e_ss, e_rs, o_ss, o_rs, l_ss, l_rs, w_ss, w_rs, g_ss, g_rs, w_ls, out_ls, in_ls,
):
    rows = q_soft.shape[0]
    width = q_soft.shape[1] // heads
    columns = weights.shape[3]
    seq = lax.axis_index("seq")
    group = lax.axis_index("head")
    z, p = seq // PLANE, seq % PLANE
    x, y = p % 2, p // 2
    places = (p, 2 * y + 1 - x, 2 * (1 - y) + x, 3 - p)
    chips = tuple(z * PLANE + place for place in places)

    def remote(src, dst, ss, rs, **device):
        return pltpu.make_async_remote_copy(
            src_ref=src, dst_ref=dst, send_sem=ss, recv_sem=rs,
            device_id=device, device_id_type=MESH,
        )

    def cols(h):
        return slice(h * width, (h + 1) * width)

    loads = [
        pltpu.make_async_copy(src, dst, in_ls.at[i])
        for i, (src, dst) in enumerate((
            (decay_hbm, decay), (k_lin_hbm, k_lin), (v_lin_hbm, v_lin), (q_lin_hbm, q_lin),
            (v_hbm, v_soft), (k_hbm, k_soft), (q_hbm, q_soft),
        ))
    ]
    for copy in loads:
        copy.start()

    barrier = pltpu.get_barrier_semaphore()
    for r in range(1, PLANE):
        pl.semaphore_signal(barrier, inc=1, device_id={"seq": chips[r]}, device_id_type=MESH)
    for k in range(1, planes):
        other = lax.rem(z + k, planes) * PLANE + p
        pl.semaphore_signal(barrier, inc=1, device_id={"seq": other}, device_id_type=MESH)
    for j in range(1, groups):
        peer = lax.rem(group + j, groups)
        pl.semaphore_signal(barrier, inc=1, device_id={"head": peer}, device_id_type=MESH)
    own_weights = []
    for layer, wo in enumerate((wo_lin, wo_soft)):
        piece = wo.at[:, pl.ds(pl.multiple_of(group * columns, 128), columns)]
        own_weights.append(
            pltpu.make_async_copy(piece, weights.at[layer, group], w_ls.at[layer])
        )
    for copy in own_weights:
        copy.start()
    pl.semaphore_wait(barrier, PLANE - 1 + planes - 1 + groups - 1)

    k_send = [remote(k_hbm, k_in.at[r - 1], k_ss.at[r - 1], k_rs.at[r - 1], seq=chips[r]) for r in (1, 2)]
    v_send = [remote(v_hbm, v_in.at[r - 1], v_ss.at[r - 1], v_rs.at[r - 1], seq=chips[r]) for r in (1, 2)]
    k_send[0].start()
    v_send[1].start()
    v_send[0].start()
    k_send[1].start()

    def query_copy(k):
        return remote(
            q_hbm, q_in.at[k - 1], q_ss.at[k - 1], q_rs.at[k - 1], seq=(z - k) * PLANE + p
        )

    for k in range(planes - 1, 0, -1):
        @pl.when(z >= k)
        def _(k=k):
            query_copy(k).start()

    weight_send = []
    for layer, wo in enumerate((wo_lin, wo_soft)):
        for j in range(1, groups):
            peer = lax.rem(group + j, groups)
            piece = wo.at[:, pl.ds(pl.multiple_of(peer * columns, 128), columns)]
            weight_send.append(
                remote(piece, weights.at[layer, group], w_ss.at[layer, j], w_rs.at[layer, j], head=peer)
            )
    for copy in weight_send:
        copy.start()

    before = lax.broadcasted_iota(jnp.int32, (rows, rows), 1)
    after = lax.broadcasted_iota(jnp.int32, (rows, rows), 0)
    lower = before <= after
    for copy in loads[:3]:
        copy.wait()
    triangle = lower.astype(F32)
    sum_row = dot(decay[...], triangle, 1, 1, HIGHEST)
    sum_col = dot(triangle, decay[...], 1, 1, HIGHEST)
    d_own[...] = jnp.zeros_like(d_own)
    for h in range(heads):
        row = sum_row[h : h + 1, :]
        total = row[:, rows - 1 : rows]
        d_own[h : h + 1, :] = jnp.broadcast_to(total, (1, width))
        faded = k_lin[:, cols(h)].astype(F32).T * jnp.exp(total - row)
        s_own[cols(h), :] = split_dot(faded, v_lin[:, cols(h)]).astype(BF16)
    s_send = [
        remote(s_own, s_in.at[r - 1], s_ss.at[r - 1], s_rs.at[r - 1], seq=chips[r])
        for r in range(1, PLANE)
    ]
    d_send = [
        remote(d_own, d_in.at[r - 1], d_ss.at[r - 1], d_rs.at[r - 1], seq=chips[r])
        for r in range(1, PLANE)
    ]
    for copy in s_send + d_send:
        copy.start()

    for copy in loads[3:]:
        copy.wait()
    for h in range(heads):
        gap = jnp.where(lower, sum_col[:, h : h + 1] - sum_row[h : h + 1, :], NEG_BIG)
        near = dot(q_lin[:, cols(h)], k_lin[:, cols(h)], 1, 1) * jnp.exp(gap)
        inside[:, cols(h)] = split_dot(near, v_lin[:, cols(h)])
    vt[0] = v_soft[...].T

    for copy in s_send + d_send:
        copy.wait_recv()
    spans = [d_own[...]] + [d_in[r] for r in range(PLANE - 1)]
    e_own[...] = sum(spans)
    for h in range(heads):
        whole = jnp.zeros((width, width), F32)
        earlier = jnp.zeros((width, width), F32)
        for r in range(PLANE):
            state = (s_own if r == 0 else s_in.at[r - 1])[cols(h), :].astype(F32)
            to_end = jnp.zeros((1, width), F32)
            to_here = jnp.zeros((1, width), F32)
            for other in range(PLANE):
                span = spans[other][h : h + 1, :]
                later = places[other] > places[r]
                to_end = to_end + jnp.where(later, span, 0.0)
                to_here = to_here + jnp.where(later & (places[other] < p), span, 0.0)
            whole = whole + jnp.exp(to_end) * state
            earlier = earlier + jnp.where(places[r] < p, jnp.exp(to_here), 0.0) * state
        t_own[cols(h), :] = whole.astype(BF16)
        carried[cols(h), :] = earlier

    def total_copies(k):
        there = (z + k) * PLANE + p
        return (
            remote(t_own, t_in.at[k - 1], t_ss.at[k - 1], t_rs.at[k - 1], seq=there),
            remote(e_own, e_in.at[k - 1], e_ss.at[k - 1], e_rs.at[k - 1], seq=there),
        )

    for k in range(1, planes):
        @pl.when(z + k < planes)
        def _(k=k):
            for copy in total_copies(k):
                copy.start()

    k_send[0].wait_recv()
    k_pass = remote(k_in.at[0], k_in.at[2], k_ss.at[2], k_rs.at[2], seq=chips[2])
    k_pass.start()
    v_send[1].wait_recv()
    v_pass = remote(v_in.at[1], v_in.at[2], v_ss.at[2], v_rs.at[2], seq=chips[1])
    v_pass.start()

    scale = factor * math.log2(math.e)

    def score(query, h, r, top=None, masked=False):
        keys = (k_soft if r == 0 else k_in.at[r - 1])[:, cols(h)]
        part = dot(keys, query, 1, 1)
        if masked:
            part = jnp.where(after <= before, part, NEG_BIG)
        scores[h, r] = part
        best = jnp.max(part, axis=0, keepdims=True)
        return best if top is None else jnp.maximum(top, best)

    def finish(h, slots, top):
        total = jnp.zeros_like(top)
        result = jnp.zeros((width, rows), F32)
        for r in slots:
            weight = jnp.exp2((scores[h, r] - top) * scale)
            total = total + jnp.sum(weight, axis=0, keepdims=True)
            result = result + dot(vt[r, cols(h), :], weight.astype(BF16))
        return result / total, top * scale + jnp.log2(total)

    def merged(mine, level_here, theirs, level_there):
        level = jnp.maximum(level_here, level_there)
        a, b = jnp.exp2(level_here - level), jnp.exp2(level_there - level)
        both = a + b
        return mine * (a / both) + theirs * (b / both), level + jnp.log2(both)

    def merge(h, theirs, level_there):
        o_self[cols(h), :], l_self[h : h + 1, :] = merged(
            o_self[cols(h), :], l_self[h : h + 1, :], theirs, level_there
        )

    for h in range(heads):
        top = score(q_soft[:, cols(h)], h, 0, masked=True)
        o_self[cols(h), :], l_self[h : h + 1, :] = finish(h, (0,), top)
    vt[2] = v_in[1].T
    v_send[0].wait_recv()
    vt[1] = v_in[0].T
    k_send[1].wait_recv()

    def last_slot():
        k_pass.wait_recv()
        v_pass.wait_recv()
        vt[3] = v_in[2].T

    def output_copies(k, h):
        there = (z + 1) * PLANE + p
        return (
            remote(
                o_out.at[k - 1, cols(h)], o_in.at[k - 1, cols(h)],
                o_ss.at[k - 1, h], o_rs.at[k - 1, h], seq=there,
            ),
            remote(
                l_out.at[k - 1, h], l_in.at[k - 1, h],
                l_ss.at[k - 1, h], l_rs.at[k - 1, h], seq=there,
            ),
        )

    for target in range(planes - 1, 0, -1):
        @pl.when(z < target)
        def _(target=target):
            k = target - z
            query_copy(k).wait_recv()
            queries = [q_in[k - 1, :, cols(h)] for h in range(heads)]
            tops = [None] * heads
            for h in range(heads):
                for r in range(PLANE - 1):
                    tops[h] = score(queries[h], h, r, tops[h])
            if target == planes - 1:
                last_slot()
            for h in range(heads):
                tops[h] = score(queries[h], h, PLANE - 1, tops[h])
                result, level = finish(h, range(PLANE), tops[h])
                o_part[k - 1, cols(h), :] = result
                l_out[k - 1, h] = jnp.broadcast_to(level, (8, rows))

                @pl.when(z == 0)
                def _(h=h, k=k):
                    o_out[k - 1, cols(h), :] = o_part[k - 1, cols(h), :].astype(BF16)
                    for copy in output_copies(k, h):
                        copy.start()

    @pl.when(z == planes - 1)
    def _():
        last_slot()

    def own_rows(chosen):
        for r in range(1, PLANE):
            @pl.when(chosen & (places[r] < p))
            def _(r=r):
                for h in range(heads):
                    top = score(q_soft[:, cols(h)], h, r)
                    merge(h, *finish(h, (r,), top))

    own_rows(z >= 2)

    for target in range(planes - 1, 1, -1):
        @pl.when((z >= 1) & (z < target))
        def _(target=target):
            k = target - z
            for h in range(heads):
                for copy in output_copies(k + 1, h):
                    copy.wait_recv()
                result, level = merged(
                    o_part[k - 1, cols(h), :], l_out[k - 1, h, 0:1, :],
                    o_in[k, cols(h), :].astype(F32), l_in[k, h, 0:1, :],
                )
                o_out[k - 1, cols(h), :] = result.astype(BF16)
                l_out[k - 1, h] = jnp.broadcast_to(level, (8, rows))
                for copy in output_copies(k, h):
                    copy.start()

    own_rows(z < 2)

    for k in range(planes - 1, 0, -1):
        @pl.when(z >= k)
        def _(k=k):
            for copy in total_copies(k):
                copy.wait_recv()
    ahead = [jnp.where(places[r] < p, spans[r], 0.0) for r in range(PLANE)]
    reach = sum(ahead)
    for k in range(1, planes):
        @pl.when(z >= k)
        def _(k=k):
            gone = reach
            for nearer in range(1, k):
                gone = gone + e_in[nearer - 1]
            for h in range(heads):
                carried[cols(h), :] += jnp.exp(gone[h : h + 1, :]) * t_in[k - 1, cols(h), :].astype(F32)
    for h in range(heads):
        state = carried[cols(h), :]
        high = state.astype(BF16)
        low = (state - high.astype(F32)).astype(BF16)
        query = q_lin[:, cols(h)]
        raw = inside[:, cols(h)] + (dot(query, high) + dot(query, low)) * jnp.exp(sum_col[:, h : h + 1])
        norm = lax.rsqrt(jnp.mean(raw * raw, axis=-1, keepdims=True) + 1e-6)
        gathered[0, group, :, cols(h)] = (raw * norm).astype(BF16)

    def exchange(layer):
        return [
            remote(
                gathered.at[layer, group], gathered.at[layer, group],
                g_ss.at[layer, j], g_rs.at[layer, j], head=lax.rem(group + j, groups),
            )
            for j in range(1, groups)
        ]

    step = min(columns, 512)

    def project_own(layer):
        for c in range(columns // step):
            piece = pl.ds(c * step, step)
            totals[:, piece] = dot(gathered[layer, group], weights[layer, group, :, piece])

    def project_others(layer, out_hbm):
        copies = []
        for c in range(columns // step):
            piece = pl.ds(c * step, step)
            total = totals[:, piece]
            for j in range(1, groups):
                g = lax.rem(group + j, groups)
                total = total + dot(gathered[layer, g], weights[layer, g, :, piece])
            staged[layer, :, piece] = total.astype(BF16)
            copy = pltpu.make_async_copy(
                staged.at[layer, :, piece], out_hbm.at[:, piece], out_ls.at[layer, c]
            )
            copy.start()
            copies.append(copy)
        return copies

    lin_send = exchange(0)
    for copy in lin_send:
        copy.start()
    for copy in own_weights:
        copy.wait()
    project_own(0)
    for copy in weight_send:
        copy.wait_recv()
    for copy in lin_send:
        copy.wait_recv()
    out_copies = project_others(0, lin_hbm)

    @pl.when(z >= 1)
    def _():
        for h in range(heads):
            for copy in output_copies(1, h):
                copy.wait_recv()
            merge(h, o_in[0, cols(h), :].astype(F32), l_in[0, h, 0:1, :])

    gathered[1, group] = o_self[...].T.astype(BF16)
    soft_send = exchange(1)
    for copy in soft_send:
        copy.start()
    project_own(1)
    for copy in soft_send:
        copy.wait_recv()
    out_copies += project_others(1, soft_hbm)

    for copy in k_send + v_send + [k_pass, v_pass] + weight_send + s_send + d_send + lin_send + soft_send:
        copy.wait_send()
    for k in range(1, planes):
        @pl.when(z >= k)
        def _(k=k):
            query_copy(k).wait_send()

        @pl.when(z + k < planes)
        def _(k=k):
            for copy in total_copies(k):
                copy.wait_send()
            for h in range(heads):
                for copy in output_copies(k, h):
                    copy.wait_send()
    for copy in out_copies:
        copy.wait()


def deliver_kernel(lin, soft, lin_out, soft_out, held, in_sem, out_sem):
    chunks = held.shape[1]
    rows = held.shape[2]
    fetch, store = [], []
    for layer, (src, dst) in enumerate(((lin, lin_out), (soft, soft_out))):
        for c in range(chunks):
            piece = pl.ds(c * rows, rows)
            fetch.append(
                pltpu.make_async_copy(src.at[piece], held.at[layer, c], in_sem.at[layer, c])
            )
            store.append(
                pltpu.make_async_copy(held.at[layer, c], dst.at[piece], out_sem.at[layer, c])
            )
    for copy in fetch:
        copy.start()
    for arrived, copy in zip(fetch, store):
        arrived.wait()
        copy.start()
    for copy in store:
        copy.wait()


def deliver(lin, soft):
    rows, columns = lin.shape
    chunks = 4
    anywhere = pl.BlockSpec(memory_space=pl.ANY)
    out = jax.ShapeDtypeStruct(lin.shape, lin.dtype)
    return pl.pallas_call(
        deliver_kernel,
        out_shape=(out, out),
        in_specs=[anywhere] * 2,
        out_specs=(anywhere, anywhere),
        scratch_shapes=[
            pltpu.VMEM((2, chunks, rows // chunks, columns), BF16),
            pltpu.SemaphoreType.DMA((2, chunks)),
            pltpu.SemaphoreType.DMA((2, chunks)),
        ],
        compiler_params=pltpu.CompilerParams(vmem_limit_bytes=60 * 1024 * 1024),
        name="deliver",
    )(lin, soft)


def local(planes, groups, *arrays):
    q_lin, _, _, decay, q_soft, _, _, wo_lin, _ = arrays
    rows, both = q_soft.shape
    heads = decay.shape[0]
    width = both // heads
    columns = wo_lin.shape[1] // groups
    far = max(planes - 1, 1)
    near = PLANE - 1
    vmem = pltpu.VMEM
    dma = pltpu.SemaphoreType.DMA
    scratch = [
        vmem((rows, both), BF16),
        vmem((rows, both), BF16),
        vmem((rows, both), BF16),
        vmem(decay.shape, F32),
        vmem((rows, both), BF16),
        vmem((rows, both), BF16),
        vmem((rows, both), BF16),
        vmem((rows, columns), F32),
        vmem((far, rows, both), BF16),
        vmem((near, rows, both), BF16),
        vmem((near, rows, both), BF16),
        vmem((PLANE, both, rows), BF16),
        vmem((heads, PLANE, rows, rows), F32),
        vmem((both, width), BF16),
        vmem((near, both, width), BF16),
        vmem((8, width), F32),
        vmem((near, 8, width), F32),
        vmem((both, width), BF16),
        vmem((far, both, width), BF16),
        vmem((8, width), F32),
        vmem((far, 8, width), F32),
        vmem((both, width), F32),
        vmem((rows, both), F32),
        vmem((far, both, rows), F32),
        vmem((far, both, rows), BF16),
        vmem((far, both, rows), BF16),
        vmem((far, heads, 8, rows), F32),
        vmem((far, heads, 8, rows), F32),
        vmem((both, rows), F32),
        vmem((8, rows), F32),
        vmem((2, groups, rows, both), BF16),
        vmem((2, groups, both, columns), BF16),
        vmem((2, rows, columns), BF16),
    ]
    pairs = [(far,)] + [(near,)] * 4 + [(far,)] * 2 + [(far, heads)] * 2
    for shape in pairs:
        scratch += [dma(shape), dma(shape)]
    for _ in range(2):
        scratch += [dma((2, groups)), dma((2, groups))]
    scratch += [dma((2,)), dma((2, columns // min(columns, 512))), dma((7,))]
    anywhere = pl.BlockSpec(memory_space=pl.ANY)
    out = jax.ShapeDtypeStruct((rows, columns), BF16)
    results = pl.pallas_call(
        functools.partial(kernel, planes, groups, heads, 1.0 / math.sqrt(width)),
        out_shape=(out, out),
        in_specs=[anywhere] * 9,
        out_specs=(anywhere, anywhere),
        scratch_shapes=scratch,
        compiler_params=pltpu.CompilerParams(
            collective_id=0, has_side_effects=True, vmem_limit_bytes=60 * 1024 * 1024
        ),
        name="attention_layers",
    )(*arrays)
    return deliver(*results)


def solution(mesh):
    planes = mesh.shape["seq"] // PLANE
    groups = mesh.shape["head"]
    in_specs = (P("seq", "head"),) * 3 + (P("head", "seq"),) + (P("seq", "head"),) * 3 + (P("head", None),) * 2
    out_specs = (P("seq", "head"), P("seq", "head"))
    return jax.shard_map(
        functools.partial(local, planes, groups),
        mesh=mesh, in_specs=in_specs, out_specs=out_specs, check_vma=False,
    )
```
